512 devices in a mesh: sea: 32 (over y, x_lo, core), fault: 16 (over z, x_hi).
Axes of the slice: x: 4 (x_hi: 2, x_lo: 2; x = x_hi * 2 + x_lo), y: 8, z: 8, core: 2. Of those that a mesh axis runs over, the one named last changes fastest.
Arguments:
- slip_rate: bfloat16 [65536, 128], P(('fault', 'sea')), may hold values from -6 to 6
- near_blocks: bfloat16 [32, 16, 8, 256, 256], P('sea', 'fault'), may hold values from -0.375 to 0.375
- near_rows: int32 [32, 16, 8], P('sea', 'fault'), may hold values from 0 to 15
- near_cols: int32 [32, 16, 8], P('sea', 'fault'), may hold values from 0 to 15
- near_scale: float32 [32, 16, 8], P('sea', 'fault'), may hold values from 0.1 to 0.5
- far_left: bfloat16 [32, 16, 24, 48, 256], P('sea', 'fault'), may hold values from -0.875 to 0.875
- far_right: bfloat16 [32, 16, 24, 48, 256], P('sea', 'fault'), may hold values from -0.375 to 0.375
- far_rows: int32 [32, 16, 24], P('sea', 'fault'), may hold values from 0 to 15
- far_cols: int32 [32, 16, 24], P('sea', 'fault'), may hold values from 0 to 15
- far_rank: int32 [32, 16, 24], P('sea', 'fault'), may hold values from 16 to 48, as said below
- far_scale: float32 [32, 16, 24], P('sea', 'fault'), may hold values from 0.1 to 0.5
- sea_depth: float32 [512, 256], P('sea', 'fault'), may hold values from 0.3 to 1
- wet_mask: int32 [512, 256], P('sea', 'fault'), may hold values 0 or 1
Outputs:
- uplift: float32 [512, 256, 128], P('sea', 'fault')
- sea_level: float32 [512, 256, 128], P('sea', 'fault')
The draws below stay inside these ranges and needn't reach their ends.
Inputs may be any that keep to these rules, and one draw needn't show every extreme that they name: `far_rank`: block 0 of every device has rank 48; every rank is at least 16.
All inputs are finite; a program needn't handle non-finite values. No bound on the sum of `wet_mask` on one device may be relied on, other than what follows from the above.
Results may differ from the reference program's by a relative error of at most 0.0024.
Values may be sent and summed in bfloat16 or wider, within the bound.
A program may use at most 64 MiB of HBM per device.

```python
import math
import jax
import jax.numpy as jnp
from jax import lax

LEAF = 256
RANK = 48
SCENARIOS = 128
BY = 16
COL_LEAVES = 16
NEAR = 8
FAR = 24
STEPS = 6
ROW_LEAVES = 16
ELEMENTS = 65536
GRID_Y = 512
GRID_X = 256
N_SEA = 32
N_FAULT = 16


def draw_far_rank(key, part):
    drawn_ranks = jax.random.randint(key, (N_SEA, N_FAULT, FAR), RANK // 3, RANK + 1)
    return drawn_ranks.at[:, :, 0].set(RANK).astype(jnp.int32)


def plant(entries, stream_key, least, largest):
    dims = entries.shape
    index_at = [jax.random.randint(jax.random.fold_in(stream_key, axis), (), 0, dims[axis]) for axis in range(len(dims))]
    entries = entries.at[tuple(index_at)].set(least)
    longest = dims.index(max(dims))
    index_at[longest] = (index_at[longest] + 1) % dims[longest]
    return entries.at[tuple(index_at)].set(largest)


def block_levels(stream_key, dims, pieces, low, top_value):
    def one(dim, blocks):
        heights = jax.random.uniform(jax.random.fold_in(jax.random.fold_in(stream_key, 6), dim), (blocks,), jnp.float32, low / len(pieces), top_value / len(pieces))
        return jnp.repeat(jnp.exp(heights), dims[dim] // blocks).reshape((-1,) + (1,) * (len(dims) - dim - 1))

    gain = one(*pieces[0])
    for cut in pieces[1:]:
        gain = gain * one(*cut)
    return gain


def noise(rng, extent, scale, most, pieces=(), dtype=jnp.bfloat16):
    entries = scale * jax.random.normal(rng, extent, jnp.float32)
    if pieces:
        entries = entries * block_levels(rng, extent, pieces, -0.22, 0.18)
    return jnp.clip(entries, -most, most).astype(dtype)


def setup_inputs(seed: int = 0) -> dict:
    arg_keys = jax.random.split(jax.random.key(seed), 14)
    slip_rate = noise(arg_keys[0], (ELEMENTS, SCENARIOS), 1.0, 6.0, ((0, 512),))
    near_blocks = noise(arg_keys[1], (N_SEA, N_FAULT, NEAR, LEAF, LEAF), LEAF ** -0.5, 0.375, ((0, 32), (1, 16)))
    near_rows = plant(jax.random.randint(arg_keys[2], (N_SEA, N_FAULT, NEAR), 0, ROW_LEAVES), jax.random.fold_in(arg_keys[2], 1), 0, ROW_LEAVES - 1).astype(jnp.int32)
    near_cols = plant(jax.random.randint(arg_keys[3], (N_SEA, N_FAULT, NEAR), 0, COL_LEAVES), jax.random.fold_in(arg_keys[3], 1), 0, COL_LEAVES - 1).astype(jnp.int32)
    near_scale = jnp.clip(jnp.exp(math.log(0.5) - 1.609438 * jax.random.uniform(arg_keys[4], (N_SEA, N_FAULT, NEAR), jnp.float32) ** block_levels(arg_keys[4], (N_SEA, N_FAULT, NEAR), ((0, 32), (1, 16)), -0.2, 0.2)), 0.1, 0.5)
    far_left = noise(arg_keys[5], (N_SEA, N_FAULT, FAR, RANK, LEAF), RANK ** -0.5, 0.875, ((0, 32), (1, 16)))
    far_right = noise(arg_keys[6], (N_SEA, N_FAULT, FAR, RANK, LEAF), LEAF ** -0.5, 0.375, ((0, 32), (1, 16)))
    far_rows = plant(jax.random.randint(arg_keys[7], (N_SEA, N_FAULT, FAR), 0, ROW_LEAVES), jax.random.fold_in(arg_keys[7], 1), 0, ROW_LEAVES - 1).astype(jnp.int32)
    far_cols = plant(jax.random.randint(arg_keys[8], (N_SEA, N_FAULT, FAR), 0, COL_LEAVES), jax.random.fold_in(arg_keys[8], 1), 0, COL_LEAVES - 1).astype(jnp.int32)
    far_rank = draw_far_rank(jax.random.fold_in(arg_keys[13], 71), 0)
    far_scale = jnp.clip(jnp.exp(math.log(0.5) - 1.609438 * jax.random.uniform(arg_keys[10], (N_SEA, N_FAULT, FAR), jnp.float32) ** block_levels(arg_keys[10], (N_SEA, N_FAULT, FAR), ((0, 32), (1, 16)), -0.2, 0.2)), 0.1, 0.5)
    sea_depth = jnp.clip(0.3 + 0.7 * jax.random.uniform(arg_keys[11], (GRID_Y, GRID_X), jnp.float32) ** block_levels(arg_keys[11], (GRID_Y, GRID_X), ((0, 32), (1, 16)), -0.2, 0.2), 0.3, 1.0)
    wet_mask = plant((jax.random.randint(arg_keys[12], (GRID_Y, GRID_X), 0, 5) < 4).astype(jnp.int32), jax.random.fold_in(arg_keys[12], 1), 0, 1)
    return dict(slip_rate=slip_rate, near_blocks=near_blocks, near_rows=near_rows, near_cols=near_cols, near_scale=near_scale, far_left=far_left, far_right=far_right, far_rows=far_rows, far_cols=far_cols, far_rank=far_rank, far_scale=far_scale, sea_depth=sea_depth, wet_mask=wet_mask)


gravity_step = 0.7
height_step = 0.7


def advance(height, east_flow, north_flow, depth_pad):
    new_east = east_flow[1:-1, :-1] - gravity_step * (height[1:-1, 1:] - height[1:-1, :-1])
    east_depth = jnp.minimum(depth_pad[1:-1, :-1], depth_pad[1:-1, 1:])
    flux_east = east_depth[:, :, None] * new_east
    new_north = north_flow[:-1, 1:-1] - gravity_step * (height[1:, 1:-1] - height[:-1, 1:-1])
    north_depth = jnp.minimum(depth_pad[:-1, 1:-1], depth_pad[1:, 1:-1])
    flux_north = north_depth[:, :, None] * new_north
    change = flux_east[:, 1:] - flux_east[:, :-1] + flux_north[1:] - flux_north[:-1]
    new_height = height[1:-1, 1:-1] - height_step * change
    return new_height, new_east[:, 1:], new_north[1:]


def cluster_uplift(inputs, leaves):
    near_blocks, near_rows, near_cols, near_scale, far_left, far_right, far_rows, far_cols, far_rank, far_scale = inputs
    fault_index = jnp.arange(N_FAULT)[:, None]
    targets = jnp.arange(ROW_LEAVES)
    near_slip = leaves[fault_index, near_cols]
    near_term = jnp.einsum('fbij,fbjs->fbis', near_blocks.astype(jnp.float32), near_slip.astype(jnp.float32))
    near_weight = (near_rows[..., None] == targets).astype(jnp.float32) * near_scale[..., None]
    total = jnp.einsum('fbr,fbis->ris', near_weight, near_term, precision=lax.Precision.HIGHEST)
    far_slip = leaves[fault_index, far_cols]
    coeffs = jnp.einsum('fbkc,fbcs->fbks', far_right.astype(jnp.float32), far_slip.astype(jnp.float32))
    kept = jnp.arange(RANK)[:, None] < far_rank[..., None, None]
    coeffs = jnp.where(kept, coeffs, jnp.float32(0.0)).astype(jnp.bfloat16)
    far_term = jnp.einsum('fbki,fbks->fbis', far_left.astype(jnp.float32), coeffs.astype(jnp.float32))
    far_weight = (far_rows[..., None] == targets).astype(jnp.float32) * far_scale[..., None]
    total = total + jnp.einsum('fbr,fbis->ris', far_weight, far_term, precision=lax.Precision.HIGHEST)
    return total.reshape(BY, GRID_X, SCENARIOS)


def reference(slip_rate, near_blocks, near_rows, near_cols, near_scale, far_left, far_right, far_rows, far_cols, far_rank, far_scale, sea_depth, wet_mask):
    leaves = slip_rate.reshape(N_FAULT, COL_LEAVES, LEAF, SCENARIOS)
    inputs = (near_blocks, near_rows, near_cols, near_scale, far_left, far_right, far_rows, far_cols, far_rank, far_scale)
    stacked = lax.map(lambda entry: cluster_uplift(entry, leaves), inputs)
    uplift = stacked.reshape(GRID_Y, GRID_X, SCENARIOS)
    wet = wet_mask.astype(jnp.float32)
    depth_pad = jnp.pad(sea_depth * wet, 1)
    height = uplift * wet[:, :, None]
    east_flow = jnp.zeros_like(height)
    north_flow = jnp.zeros_like(height)
    margin = ((1, 1), (1, 1), (0, 0))
    for step_index in range(STEPS):
        height, east_flow, north_flow = advance(jnp.pad(height, margin), jnp.pad(east_flow, margin), jnp.pad(north_flow, margin), depth_pad)
    return uplift, height
```

```python
import jax
import jax.numpy as jnp
from jax import lax
from jax.experimental import pallas as pl
from jax.experimental.pallas import tpu as pltpu
from jax.sharding import PartitionSpec as P

STEPS = 6
GRAVITY_STEP = 0.7
HEIGHT_STEP = 0.7
GAIN = GRAVITY_STEP * HEIGHT_STEP
MESH = pl.DeviceIdType.MESH
F32, BF16 = jnp.float32, jnp.bfloat16

SEA, FAULT = 32, 16
LEAF, MEMBERS, RANK = 256, 128, 48
NEAR, FAR, LEAVES = 8, 24, 16
BRICK = 16
ROWS, COLS = BRICK + 2 * STEPS, BRICK + 16
TOP, LEFT = STEPS, 8
NEIGHBOURS = [(dy, dx) for dy in (-1, 0, 1) for dx in (-1, 0, 1) if (dy, dx) != (0, 0)]
RING = (1, 7, 2, 6, 3, 5, 4)
GROUP = 4


def mod(a, n):
    return lax.rem(a + n, n)


def kernel(
    slip, near_hbm, near_rows, near_cols, near_scale, left_hbm, right_hbm, far_rows, far_cols, far_rank, far_scale, depth, wet,
    uplift, level,
    slips, near, left, right, coeffs, acc, chain, last, x_out, x_in, z_out, z_in, depths, compact, wets, east, north, h, e, n,
    load_sem, y_send, y_recv, x_send, x_recv, c_send, c_recv, k_send, k_recv, d_send, d_recv,
    p_send, p_recv, z_send, z_recv, h_send, h_recv,
):
    s, f = lax.axis_index("sea"), lax.axis_index("fault")
    y, x_lo, core = s // 4, (s // 2) % 2, s % 2
    z, x_hi = f // 2, f % 2
    core_mate, x_mate = s + 1 - 2 * core, s + 2 - 4 * x_lo
    far_mate = f + 1 - 2 * x_hi

    def copy(src, dst, send, recv, to_sea, to_fault):
        return pltpu.make_async_remote_copy(
            src_ref=src, dst_ref=dst, send_sem=send, recv_sem=recv, device_id=(to_sea, to_fault), device_id_type=MESH
        )

    barrier = pltpu.get_barrier_semaphore()
    partners = [(mod(s + 4 * d, SEA), f) for d in RING]
    partners += [(core_mate, f), (x_mate, f), (s, far_mate)]
    partners += [(s, mod(f + 2 * d, FAULT)) for d in RING]
    partners += [(mod(s + dy, SEA), mod(f + dx, FAULT)) for dy, dx in NEIGHBOURS]
    for partner in partners:
        pl.semaphore_signal(barrier, inc=1, device_id=partner, device_id_type=MESH)
    loads = [
        pltpu.make_async_copy(src.at[0, 0], dst, load_sem.at[i])
        for i, (src, dst) in enumerate(((right_hbm, right), (near_hbm, near), (left_hbm, left)))
    ]
    for load in loads:
        load.start()
    pl.semaphore_wait(barrier, len(partners))

    def slot(index):
        return slips.at[index // 2, pl.ds(pl.multiple_of((index % 2) * 128, 128), 128), :]

    def along_y(d, back):
        return copy(slip, slot(mod(s - 4 * d, SEA) if back else s), y_send.at[d], y_recv.at[d], mod(s + 4 * d, SEA), f)

    def to_mate(d, mate, send, recv, back):
        mine = mod(s - 4 * d, SEA)
        theirs = mod(mate - 4 * d, SEA)
        src = slip if d == 0 else slot(mine)
        return copy(src, slot(theirs if back else mine), send.at[d], recv.at[d], mate, f)

    def onward(d, back):
        mine = mod(x_mate - 4 * d, SEA)
        theirs = mod(s + 1 - 2 * core + 2 - 4 * x_lo - 4 * d, SEA)
        return copy(slot(mine), slot(theirs if back else mine), k_send.at[d], k_recv.at[d], core_mate, f)

    for d in RING:
        along_y(d, False).start()
    to_mate(0, x_mate, x_send, x_recv, False).start()
    to_mate(0, core_mate, c_send, c_recv, False).start()
    slips[s // 2, pl.ds(pl.multiple_of((s % 2) * 128, 128), 128), :] = slip[...]

    wet_here = wet[...].astype(F32)
    depths[4] = jnp.zeros((BRICK, 128), F32)
    depths[4, :, :BRICK] = depth[...] * wet_here

    def depth_copy(i):
        dy, dx = NEIGHBOURS[i]
        k = (dy + 1) * 3 + dx + 1
        return copy(depths.at[4], depths.at[k], d_send.at[i], d_recv.at[i], mod(s - dy, SEA), mod(f - dx, FAULT))

    for i in range(8):
        depth_copy(i).start()

    acc[0] = jnp.zeros((LEAF, MEMBERS), F32)
    for r in range(LEAVES):
        last[r] = 0

    def link(rows, first):
        def body(b, carry):
            row = rows[0, 0, b]
            chain[first + b] = last[row]
            for r in range(LEAVES):
                last[r] = jnp.where(row == r, first + b, last[r])
            return carry

        return body

    lax.fori_loop(0, NEAR, link(near_rows, 1), 0)
    lax.fori_loop(0, FAR, link(far_rows, 1 + NEAR), 0)

    before = 0
    for d in RING:
        along_y(d, True).wait_recv()
        to_mate(d, x_mate, x_send, x_recv, False).start()
        to_mate(d, core_mate, c_send, c_recv, False).start()
        to_mate(before, x_mate, x_send, x_recv, True).wait_recv()
        onward(before, False).start()
        before = d
    to_mate(before, x_mate, x_send, x_recv, True).wait_recv()
    onward(before, False).start()

    lane = lax.broadcasted_iota(jnp.int32, (BRICK, 128), 1)
    for i in range(8):
        depth_copy(i).wait_recv()
    west_ok, east_ok = f > 0, f < FAULT - 1
    for dy, place in ((-1, 0), (0, TOP), (1, TOP + BRICK)):
        row_ok = (s + dy >= 0) & (s + dy < SEA)
        k = (dy + 1) * 3
        west = jnp.where((lane >= 8) & (lane < 16) & west_ok, depths[k], 0.0)
        east_side = jnp.where((lane < 8) & east_ok, depths[k + 2], 0.0)
        band = pltpu.roll(west, 120, 1) + pltpu.roll(depths[k + 1], 8, 1) + pltpu.roll(east_side, 24, 1)
        band = jnp.where(row_ok, band, 0.0)
        rows = band[BRICK - STEPS :] if dy < 0 else band[:STEPS] if dy > 0 else band
        compact[place : place + rows.shape[0], :] = rows
    eye = lax.broadcasted_iota(jnp.int32, (COLS, 128), 1) == lax.broadcasted_iota(jnp.int32, (COLS, 128), 0)

    def spread(row, width):
        kept = jnp.where(eye[:width], jnp.broadcast_to(row, (width, 128)), 0.0)
        return jnp.broadcast_to(jnp.sum(kept, axis=1, keepdims=True), (width, 128))

    def edges(i, carry):
        here = compact[pl.ds(i, 1), :]
        east[i] = spread(GAIN * jnp.minimum(here, pltpu.roll(here, 127, 1)), COLS)
        north[i] = spread(GAIN * jnp.minimum(here, compact[pl.ds(i + 1, 1), :]), COLS)
        return carry

    compact[ROWS:, :] = jnp.zeros((compact.shape[0] - ROWS, 128), F32)
    lax.fori_loop(0, ROWS, edges, 0)
    depths[9] = jnp.zeros((BRICK, 128), F32)
    depths[9, :, :BRICK] = wet_here

    def dry(i, carry):
        wets[i] = spread(depths[9, pl.ds(i, 1), :], BRICK)
        return carry

    for i in range(8):
        depth_copy(i).wait_send()
    lax.fori_loop(0, BRICK, dry, 0)

    for load in loads:
        load.wait()
    for d in (0,) + RING:
        to_mate(d, core_mate, c_send, c_recv, True).wait_recv()
        onward(d, True).wait_recv()

    rank_of = lax.broadcasted_iota(jnp.int32, (RANK, MEMBERS), 0)

    def project(g, carry):
        for i in range(GROUP):
            b = g * GROUP + i
            made = jnp.dot(right[b], slips[far_cols[0, 0, b]], preferred_element_type=F32)
            coeffs[b] = jnp.where(rank_of < far_rank[0, 0, b], made, 0.0).astype(BF16)
        return carry

    def near_sum(g, carry):
        for i in range(GROUP):
            b = g * GROUP + i
            term = jnp.dot(near[b], slips[near_cols[0, 0, b]], preferred_element_type=F32)
            acc[1 + b] = term * near_scale[0, 0, b] + acc[chain[1 + b]]
        return carry

    def far_sum(g, carry):
        for i in range(GROUP):
            b = g * GROUP + i
            term = lax.dot_general(left[b], coeffs[b], (((0,), (0,)), ((), ())), preferred_element_type=F32)
            acc[1 + NEAR + b] = term * far_scale[0, 0, b] + acc[chain[1 + NEAR + b]]
        return carry

    lax.fori_loop(0, FAR // GROUP, project, 0)
    lax.fori_loop(0, NEAR // GROUP, near_sum, 0)
    lax.fori_loop(0, FAR // GROUP, far_sum, 0)

    def offset(j):
        return 4 + ((j + 1) // 2) * (1 - 2 * (j % 2))

    def part(j, half, r):
        owner = 2 * mod(z + offset(j), 8) + half
        return acc[last[r], pl.ds(pl.multiple_of(owner * BRICK, BRICK), BRICK), :]

    def pair(j):
        return copy(x_out.at[j], x_in.at[j], p_send.at[j], p_recv.at[j], s, far_mate)

    def along_z(j):
        return copy(z_out.at[j], z_in.at[j], z_send.at[j], z_recv.at[j], s, 2 * mod(z + offset(j), 8) + x_hi)

    def send_pair(j, carry):
        for r in range(BRICK):
            x_out[j, r] = part(j, 1 - x_hi, r).astype(BF16)
        pair(j).start()
        return carry

    def send_z(j, carry):
        pair(j).wait_recv()
        for r in range(BRICK):
            z_out[j, r] = (part(j, x_hi, r) + x_in[j, r].astype(F32)).astype(BF16)
        along_z(j).start()
        return carry

    def add_z(j, carry):
        along_z(j).wait_recv()
        for r in range(BRICK):
            uplift[r] = uplift[r] + z_in[j, r].astype(F32)
        return carry

    lax.fori_loop(0, 8, send_pair, 0)
    lax.fori_loop(0, 7, send_z, 0)
    pair(7).wait_recv()
    for r in range(BRICK):
        uplift[r] = part(7, x_hi, r) + x_in[7, r].astype(F32)
    lax.fori_loop(0, 7, add_z, 0)
    for r in range(BRICK):
        h[TOP + r, LEFT : LEFT + BRICK, :] = uplift[r] * wets[r]

    def halo(i):
        dy, dx = NEIGHBOURS[i]
        tall, wide = (BRICK if dy == 0 else STEPS), (BRICK if dx == 0 else 8)
        src_y, dst_y = {-1: (TOP + BRICK - STEPS, 0), 0: (TOP, TOP), 1: (TOP, TOP + BRICK)}[dy]
        src_x, dst_x = {-1: (LEFT + BRICK - 8, 0), 0: (LEFT, LEFT), 1: (LEFT, LEFT + BRICK)}[dx]
        return copy(
            h.at[src_y : src_y + tall, src_x : src_x + wide, :],
            h.at[dst_y : dst_y + tall, dst_x : dst_x + wide, :],
            h_send.at[i], h_recv.at[i], mod(s - dy, SEA), mod(f - dx, FAULT),
        )

    for i in range(8):
        halo(i).start()
    e[...] = jnp.zeros(e.shape, F32)
    n[...] = jnp.zeros(n.shape, F32)
    for d in RING:
        along_y(d, False).wait_send()
    for d in (0,) + RING:
        to_mate(d, x_mate, x_send, x_recv, False).wait_send()
        to_mate(d, core_mate, c_send, c_recv, False).wait_send()
        onward(d, False).wait_send()
    for j in range(8):
        pair(j).wait_send()
    for j in range(7):
        along_z(j).wait_send()
    for i in range(8):
        halo(i).wait()

    for step in range(STEPS):

        def row(i, below):
            here = h[i]
            flow_n = n[i] + (h[i + 1] - here)
            flow_e = e[i] + (pltpu.roll(here, COLS - 1, 0) - here)
            n[i] = flow_n
            e[i] = flow_e
            flux_n = north[i] * flow_n
            flux_e = east[i] * flow_e
            h[i] = here + (flux_e - pltpu.roll(flux_e, 1, 0) + flux_n - below)
            return flux_n

        def first(i):
            flow_n = n[i] + (h[i + 1] - h[i])
            n[i] = flow_n
            return north[i] * flow_n

        lax.fori_loop(step + 1, ROWS - 1 - step, row, first(step))
    level[...] = h[TOP : TOP + BRICK, LEFT : LEFT + BRICK, :]


def on_device(*args):
    vmem = pl.BlockSpec(memory_space=pltpu.VMEM)
    smem = pl.BlockSpec(memory_space=pltpu.SMEM)
    hbm = pl.BlockSpec(memory_space=pl.ANY)
    field = pltpu.VMEM((ROWS, COLS, MEMBERS), F32)
    dma = pltpu.SemaphoreType.DMA
    brick = jax.ShapeDtypeStruct((BRICK, BRICK, MEMBERS), F32)
    return pl.pallas_call(
        kernel,
        out_shape=(brick, brick),
        in_specs=[vmem, hbm, smem, smem, smem, hbm, hbm, smem, smem, smem, smem, vmem, vmem],
        out_specs=(vmem, vmem),
        scratch_shapes=[
            pltpu.VMEM((LEAVES, LEAF, MEMBERS), BF16),
            pltpu.VMEM((NEAR, LEAF, LEAF), BF16),
            pltpu.VMEM((FAR, RANK, LEAF), BF16),
            pltpu.VMEM((FAR, RANK, LEAF), BF16),
            pltpu.VMEM((FAR, RANK, MEMBERS), BF16),
            pltpu.VMEM((1 + NEAR + FAR, LEAF, MEMBERS), F32),
            pltpu.SMEM((1 + NEAR + FAR,), jnp.int32),
            pltpu.SMEM((LEAVES,), jnp.int32),
            pltpu.VMEM((8, BRICK, BRICK, MEMBERS), BF16),
            pltpu.VMEM((8, BRICK, BRICK, MEMBERS), BF16),
            pltpu.VMEM((7, BRICK, BRICK, MEMBERS), BF16),
            pltpu.VMEM((7, BRICK, BRICK, MEMBERS), BF16),
            pltpu.VMEM((10, BRICK, 128), F32),
            pltpu.VMEM((32, 128), F32),
            pltpu.VMEM((BRICK, BRICK, MEMBERS), F32),
            field, field, field, field, field,
            dma((3,)),
            dma((8,)), dma((8,)), dma((8,)), dma((8,)), dma((8,)), dma((8,)), dma((8,)), dma((8,)),
            dma((8,)), dma((8,)),
            dma((8,)), dma((8,)), dma((7,)), dma((7,)), dma((8,)), dma((8,)),
        ],
        compiler_params=pltpu.CompilerParams(
            collective_id=0, has_side_effects=True, vmem_limit_bytes=48 * 2**20
        ),
        name="forecast",
    )(*args)


def solution(mesh):
    blocks = P("sea", "fault", None, None, None)
    lists = P("sea", "fault", None)
    cells = P("sea", "fault")
    return jax.shard_map(
        on_device,
        mesh=mesh,
        in_specs=(
            P(("fault", "sea"), None), blocks, lists, lists, lists, blocks, blocks, lists, lists, lists, lists, cells, cells,
        ),
        out_specs=(lists, lists),
        check_vma=False,
    )
```

```python
import jax
import jax.numpy as jnp
from jax import lax
from jax.experimental import pallas as pl
from jax.experimental.pallas import tpu as pltpu
from jax.sharding import PartitionSpec as P

STEPS = 6
GRAVITY_STEP = 0.7
HEIGHT_STEP = 0.7
GAIN = GRAVITY_STEP * HEIGHT_STEP
MESH = pl.DeviceIdType.MESH
F32, BF16 = jnp.float32, jnp.bfloat16

SEA, FAULT = 32, 16
LEAF, MEMBERS, RANK = 256, 128, 48
NEAR, FAR, LEAVES = 8, 24, 16
BRICK = 16
ROWS, COLS = BRICK + 2 * STEPS, BRICK + 16
TOP, LEFT = STEPS, 8
NEIGHBOURS = [(dy, dx) for dy in (-1, 0, 1) for dx in (-1, 0, 1) if (dy, dx) != (0, 0)]
RING = (1, 7, 2, 6, 3, 5, 4)
GROUP = 8
FAR_GROUP = 24
DIRECT = (4,)
LAG = 4


def mod(a, n):
    return lax.rem(a + n, n)


def kernel(
    slip_hbm, near_hbm, near_rows_hbm, near_cols_hbm, near_scale_hbm, left_hbm, right_hbm, far_rows_hbm, far_cols_hbm,
    far_rank_hbm, far_scale_hbm, depth_hbm, wet_hbm,
    both_hbm,
    uplift, slip, near_rows, near_cols, near_scale, far_rows, far_cols, far_rank, far_scale, depth, wet,
    slips, near, left, right, coeffs, acc, chain, last, x_out, x_in, z_out, z_in, depths, compact, wets, strip_out, strip_in, east, north, h, e, n,
    load_sem, y_send, y_recv, x_send, x_recv, c_send, c_recv, k_send, k_recv, d_send, d_recv,
    p_send, p_recv, z_send, z_recv, h_send, h_recv, out_sem,
):
    s, f = lax.axis_index("sea"), lax.axis_index("fault")
    y, x_lo, core = s // 4, (s // 2) % 2, s % 2
    z, x_hi = f // 2, f % 2
    core_mate, x_mate = s + 1 - 2 * core, s + 2 - 4 * x_lo
    far_mate = f + 1 - 2 * x_hi

    def copy(src, dst, send, recv, to_sea, to_fault):
        return pltpu.make_async_remote_copy(
            src_ref=src, dst_ref=dst, send_sem=send, recv_sem=recv, device_id=(to_sea, to_fault), device_id_type=MESH
        )

    barrier = pltpu.get_barrier_semaphore()
    partners = [(mod(s + 4 * d, SEA), f) for d in RING]
    partners += [(mod(x_mate + 4 * d, SEA), f) for d in DIRECT]
    partners += [(core_mate, f), (x_mate, f), (s, far_mate)]
    partners += [(s, mod(f + 2 * d, FAULT)) for d in RING]
    partners += [(mod(s + dy, SEA), mod(f + dx, FAULT)) for dy, dx in NEIGHBOURS]
    for partner in partners:
        pl.semaphore_signal(barrier, inc=1, device_id=partner, device_id_type=MESH)
    pairs = (
        (slip_hbm, slip), (depth_hbm, depth), (wet_hbm, wet), (near_rows_hbm, near_rows), (far_rows_hbm, far_rows),
        (near_cols_hbm, near_cols), (far_cols_hbm, far_cols), (far_rank_hbm, far_rank),
        (near_scale_hbm, near_scale), (far_scale_hbm, far_scale),
        (right_hbm.at[0, 0], right), (near_hbm.at[0, 0], near), (left_hbm.at[0, 0], left),
    )
    loads = [pltpu.make_async_copy(src, dst, load_sem.at[i]) for i, (src, dst) in enumerate(pairs)]
    for load in loads:
        load.start()
    for load in loads[:3]:
        load.wait()
    pl.semaphore_wait(barrier, len(partners))

    def slot(index):
        return slips.at[index // 2, pl.ds(pl.multiple_of((index % 2) * 128, 128), 128), :]

    def along_y(d, back):
        return copy(slip, slot(mod(s - 4 * d, SEA) if back else s), y_send.at[d], y_recv.at[d], mod(s + 4 * d, SEA), f)

    def to_mate(d, mate, send, recv, back):
        mine = mod(s - 4 * d, SEA)
        theirs = mod(mate - 4 * d, SEA)
        src = slip if d == 0 else slot(mine)
        return copy(src, slot(theirs if back else mine), send.at[d], recv.at[d], mate, f)

    def across(d):
        return copy(slip, slot(s), x_send.at[d], x_recv.at[d], mod(x_mate + 4 * d, SEA), f)

    def onward(d, back):
        mine = mod(x_mate - 4 * d, SEA)
        theirs = mod(s + 1 - 2 * core + 2 - 4 * x_lo - 4 * d, SEA)
        return copy(slot(mine), slot(theirs if back else mine), k_send.at[d], k_recv.at[d], core_mate, f)

    for d in RING:
        along_y(d, False).start()
        if d in DIRECT:
            across(d).start()
    to_mate(0, x_mate, x_send, x_recv, False).start()
    to_mate(0, core_mate, c_send, c_recv, False).start()
    slips[s // 2, pl.ds(pl.multiple_of((s % 2) * 128, 128), 128), :] = slip[...]

    wet_here = wet[...].astype(F32)
    depths[4] = jnp.zeros((BRICK, 128), F32)
    depths[4, :, :BRICK] = depth[...] * wet_here

    def depth_copy(i):
        dy, dx = NEIGHBOURS[i]
        k = (dy + 1) * 3 + dx + 1
        return copy(depths.at[4], depths.at[k], d_send.at[i], d_recv.at[i], mod(s - dy, SEA), mod(f - dx, FAULT))

    for i in range(8):
        depth_copy(i).start()

    acc[0] = jnp.zeros((LEAF, MEMBERS), F32)
    for r in range(LEAVES):
        last[r] = 0

    def link(rows, first):
        def body(b, carry):
            row = rows[0, 0, b]
            chain[first + b] = last[row]
            for r in range(LEAVES):
                last[r] = jnp.where(row == r, first + b, last[r])
            return carry

        return body

    for load in loads[3:10]:
        load.wait()
    lax.fori_loop(0, NEAR, link(near_rows, 1), 0)
    lax.fori_loop(0, FAR, link(far_rows, 1 + NEAR), 0)

    def ready(d):
        to_mate(d, x_mate, x_send, x_recv, True).wait_recv()
        onward(d, False).start()

    arrived = [0]
    for d in RING:
        along_y(d, True).wait_recv()
        if d not in DIRECT:
            to_mate(d, x_mate, x_send, x_recv, False).start()
        to_mate(d, core_mate, c_send, c_recv, False).start()
        arrived.append(d)
        if len(arrived) > LAG:
            ready(arrived.pop(0))
    for d in arrived:
        ready(d)

    for load in loads[10:]:
        load.wait()
    for d in (0,) + RING:
        to_mate(d, core_mate, c_send, c_recv, True).wait_recv()
        onward(d, True).wait_recv()

    rank_of = lax.broadcasted_iota(jnp.int32, (RANK, MEMBERS), 0)

    def project(g, carry):
        for i in range(FAR_GROUP):
            b = g * FAR_GROUP + i
            made = jnp.dot(right[b], slips[far_cols[0, 0, b]], preferred_element_type=F32)
            coeffs[b] = jnp.where(rank_of < far_rank[0, 0, b], made, 0.0).astype(BF16)
        return carry

    def near_sum(g, carry):
        for i in range(GROUP):
            b = g * GROUP + i
            term = jnp.dot(near[b], slips[near_cols[0, 0, b]], preferred_element_type=F32)
            acc[1 + b] = term * near_scale[0, 0, b] + acc[chain[1 + b]]
        return carry

    def far_sum(g, carry):
        for i in range(FAR_GROUP):
            b = g * FAR_GROUP + i
            term = lax.dot_general(left[b], coeffs[b], (((0,), (0,)), ((), ())), preferred_element_type=F32)
            acc[1 + NEAR + b] = term * far_scale[0, 0, b] + acc[chain[1 + NEAR + b]]
        return carry

    lax.fori_loop(0, FAR // FAR_GROUP, project, 0)
    lax.fori_loop(0, NEAR // GROUP, near_sum, 0)
    lax.fori_loop(0, FAR // FAR_GROUP, far_sum, 0)

    def offset(j):
        return 4 + ((j + 1) // 2) * (1 - 2 * (j % 2))

    def part(j, half, r):
        owner = 2 * mod(z + offset(j), 8) + half
        return acc[last[r], pl.ds(pl.multiple_of(owner * BRICK, BRICK), BRICK), :]

    def pair(j):
        return copy(x_out.at[j], x_in.at[j], p_send.at[j], p_recv.at[j], s, far_mate)

    def along_z(j):
        return copy(z_out.at[j], z_in.at[j], z_send.at[j], z_recv.at[j], s, 2 * mod(z + offset(j), 8) + x_hi)

    def send_pair(j, carry):
        for r in range(BRICK):
            x_out[j, r] = part(j, 1 - x_hi, r).astype(BF16)
        pair(j).start()
        return carry

    def send_z(j, carry):
        pair(j).wait_recv()
        for r in range(BRICK):
            z_out[j, r] = (part(j, x_hi, r) + x_in[j, r].astype(F32)).astype(BF16)
        along_z(j).start()
        return carry

    def geometry(j, carry):
        for i in range(4):
            edges(4 * j + i)
        for i in range(3):
            wets[3 * j + i] = spread(compact[1, pl.ds(3 * j + i, 1), :], BRICK)
        return carry

    def add_z(j, carry):
        along_z(j).wait_recv()
        for r in range(BRICK):
            uplift[r] = uplift[r] + z_in[j, r].astype(F32)
        return carry

    lax.fori_loop(0, 8, send_pair, 0)
    for i in range(8):
        depth_copy(i).wait_recv()
    lane = lax.broadcasted_iota(jnp.int32, (BRICK, 128), 1)
    west_ok, east_ok = f > 0, f < FAULT - 1
    for dy, place in ((-1, 0), (0, TOP), (1, TOP + BRICK)):
        row_ok = (s + dy >= 0) & (s + dy < SEA)
        k = (dy + 1) * 3
        west = jnp.where((lane >= 8) & (lane < 16) & west_ok, depths[k], 0.0)
        east_side = jnp.where((lane < 8) & east_ok, depths[k + 2], 0.0)
        band = pltpu.roll(west, 120, 1) + pltpu.roll(depths[k + 1], 8, 1) + pltpu.roll(east_side, 24, 1)
        band = jnp.where(row_ok, band, 0.0)
        rows = band[BRICK - STEPS :] if dy < 0 else band[:STEPS] if dy > 0 else band
        compact[0, place : place + rows.shape[0], :] = rows
    compact[0, ROWS:, :] = jnp.zeros((32 - ROWS, 128), F32)
    compact[1] = jnp.zeros((32, 128), F32)
    compact[1, :BRICK, :BRICK] = wet_here
    eye = lax.broadcasted_iota(jnp.int32, (COLS, 128), 1) == lax.broadcasted_iota(jnp.int32, (COLS, 128), 0)

    def spread(row, width):
        kept = jnp.where(eye[:width], jnp.broadcast_to(row, (width, 128)), 0.0)
        return jnp.broadcast_to(jnp.sum(kept, axis=1, keepdims=True), (width, 128))

    def edges(i):
        here = compact[0, pl.ds(i, 1), :]
        east[i] = spread(GAIN * jnp.minimum(here, pltpu.roll(here, 127, 1)), COLS)
        north[i] = spread(GAIN * jnp.minimum(here, compact[0, pl.ds(i + 1, 1), :]), COLS)

    lax.fori_loop(0, 7, send_z, 0)
    lax.fori_loop(0, 7, geometry, 0)
    pair(7).wait_recv()
    for r in range(BRICK):
        uplift[r] = part(7, x_hi, r) + x_in[7, r].astype(F32)
    lax.fori_loop(0, 7, add_z, 0)
    out_uplift = pltpu.make_async_copy(uplift, both_hbm.at[0], out_sem.at[0])
    out_uplift.start()
    for r in range(BRICK):
        h[TOP + r, LEFT : LEFT + BRICK, :] = uplift[r] * wets[r]

    def span(i):
        dy, dx = NEIGHBOURS[i]
        tall, wide = (BRICK if dy == 0 else STEPS), (BRICK if dx == 0 else 8)
        src_y, dst_y = {-1: (TOP + BRICK - STEPS, 0), 0: (TOP, TOP), 1: (TOP, TOP + BRICK)}[dy]
        src_x, dst_x = {-1: (LEFT + BRICK - 8, 0), 0: (LEFT, LEFT), 1: (LEFT, LEFT + BRICK)}[dx]
        rows = 8 * tall
        src = (slice(src_y, src_y + tall), slice(src_x, src_x + wide), slice(None))
        dst = (slice(dst_y, dst_y + tall), slice(dst_x, dst_x + wide), slice(None))
        return dx, rows, src, dst

    def halo(i):
        dy, dx = NEIGHBOURS[i]
        _, rows, src, dst = span(i)
        to_sea, to_fault = mod(s - dy, SEA), mod(f - dx, FAULT)
        if dx == 0:
            return copy(h.at[src], h.at[dst], h_send.at[i], h_recv.at[i], to_sea, to_fault)
        return copy(strip_out.at[i, :rows], strip_in.at[i, :rows], h_send.at[i], h_recv.at[i], to_sea, to_fault)

    for i in range(8):
        dx, rows, src, _ = span(i)
        if dx:
            strip_out[i, :rows] = h[src].reshape(rows, MEMBERS).astype(BF16)
        halo(i).start()
    e[...] = jnp.zeros(e.shape, F32)
    n[...] = jnp.zeros(n.shape, F32)
    for d in RING:
        along_y(d, False).wait_send()
    for d in (0,) + RING:
        to_mate(d, x_mate, x_send, x_recv, False).wait_send()
        to_mate(d, core_mate, c_send, c_recv, False).wait_send()
        onward(d, False).wait_send()
    for i in range(8):
        depth_copy(i).wait_send()
    for j in range(8):
        pair(j).wait_send()
    for j in range(7):
        along_z(j).wait_send()
    for i in range(8):
        dx, rows, _, dst = span(i)
        halo(i).wait()
        if dx:
            h[dst] = strip_in[i, :rows].astype(F32).reshape(rows // 8, 8, MEMBERS)

    for step in range(STEPS):

        def row(i, below):
            here = h[i]
            flow_n = n[i] + (h[i + 1] - here)
            flow_e = e[i] + (pltpu.roll(here, COLS - 1, 0) - here)
            n[i] = flow_n
            e[i] = flow_e
            flux_n = north[i] * flow_n
            flux_e = east[i] * flow_e
            h[i] = here + (flux_e - pltpu.roll(flux_e, 1, 0) + flux_n - below)
            return flux_n

        def first(i):
            flow_n = n[i] + (h[i + 1] - h[i])
            n[i] = flow_n
            return north[i] * flow_n

        lax.fori_loop(step + 1, ROWS - 1 - step, row, first(step))
    out_level = pltpu.make_async_copy(h.at[TOP : TOP + BRICK, LEFT : LEFT + BRICK, :], both_hbm.at[1], out_sem.at[1])
    out_level.start()
    out_level.wait()
    out_uplift.wait()


def on_device(*args):
    hbm = pl.BlockSpec(memory_space=pltpu.HBM)
    field = pltpu.VMEM((ROWS, COLS, MEMBERS), F32)
    dma = pltpu.SemaphoreType.DMA
    brick = jax.ShapeDtypeStruct((BRICK, BRICK, MEMBERS), F32)
    made = pl.pallas_call(
        kernel,
        out_shape=jax.ShapeDtypeStruct((2, BRICK, BRICK, MEMBERS), F32),
        in_specs=[hbm] * 13,
        out_specs=hbm,
        scratch_shapes=[
            pltpu.VMEM((BRICK, BRICK, MEMBERS), F32),
            pltpu.VMEM((128, MEMBERS), BF16),
            *(pltpu.SMEM((1, 1, NEAR), kind) for kind in (jnp.int32, jnp.int32, F32)),
            *(pltpu.SMEM((1, 1, FAR), kind) for kind in (jnp.int32, jnp.int32, jnp.int32, F32)),
            pltpu.VMEM((BRICK, BRICK), F32),
            pltpu.VMEM((BRICK, BRICK), jnp.int32),
            pltpu.VMEM((LEAVES, LEAF, MEMBERS), BF16),
            pltpu.VMEM((NEAR, LEAF, LEAF), BF16),
            pltpu.VMEM((FAR, RANK, LEAF), BF16),
            pltpu.VMEM((FAR, RANK, LEAF), BF16),
            pltpu.VMEM((FAR, RANK, MEMBERS), BF16),
            pltpu.VMEM((1 + NEAR + FAR, LEAF, MEMBERS), F32),
            pltpu.SMEM((1 + NEAR + FAR,), jnp.int32),
            pltpu.SMEM((LEAVES,), jnp.int32),
            pltpu.VMEM((8, BRICK, BRICK, MEMBERS), BF16),
            pltpu.VMEM((8, BRICK, BRICK, MEMBERS), BF16),
            pltpu.VMEM((7, BRICK, BRICK, MEMBERS), BF16),
            pltpu.VMEM((7, BRICK, BRICK, MEMBERS), BF16),
            pltpu.VMEM((9, BRICK, 128), F32),
            pltpu.VMEM((2, 32, 128), F32),
            pltpu.VMEM((21, BRICK, MEMBERS), F32),
            pltpu.VMEM((8, 8 * BRICK, MEMBERS), BF16), pltpu.VMEM((8, 8 * BRICK, MEMBERS), BF16),
            field, field, field, field, field,
            dma((13,)),
            dma((8,)), dma((8,)), dma((8,)), dma((8,)), dma((8,)), dma((8,)), dma((8,)), dma((8,)),
            dma((8,)), dma((8,)),
            dma((8,)), dma((8,)), dma((7,)), dma((7,)), dma((8,)), dma((8,)), dma((2,)),
        ],
        compiler_params=pltpu.CompilerParams(
            collective_id=0, has_side_effects=True, vmem_limit_bytes=62 * 2**20
        ),
        name="forecast",
    )(*args)
    return made[0], made[1]


def solution(mesh):
    blocks = P("sea", "fault", None, None, None)
    lists = P("sea", "fault", None)
    cells = P("sea", "fault")
    return jax.shard_map(
        on_device,
        mesh=mesh,
        in_specs=(
            P(("fault", "sea"), None), blocks, lists, lists, lists, blocks, blocks, lists, lists, lists, lists, cells, cells,
        ),
        out_specs=(lists, lists),
        check_vma=False,
    )
```

```python
import jax
import jax.numpy as jnp
from jax import lax
from jax.experimental import pallas as pl
from jax.experimental.pallas import tpu as pltpu
from jax.sharding import PartitionSpec as P

STEPS = 6
GRAVITY_STEP = 0.7
HEIGHT_STEP = 0.7
GAIN = GRAVITY_STEP * HEIGHT_STEP
MESH = pl.DeviceIdType.MESH
F32, BF16 = jnp.float32, jnp.bfloat16

SEA, FAULT = 32, 16
LEAF, MEMBERS, RANK = 256, 128, 48
NEAR, FAR, LEAVES = 8, 24, 16
BRICK = 16
ROWS, COLS = BRICK + 2 * STEPS, BRICK + 16
TOP, LEFT = STEPS, 8
NEIGHBOURS = [(dy, dx) for dy in (-1, 0, 1) for dx in (-1, 0, 1) if (dy, dx) != (0, 0)]
RING = (1, 7, 2, 6, 3, 5, 4)
TALL = 4
FAR_GROUP = 24
DIRECT = (4,)
LAG = 4


def mod(a, n):
    return lax.rem(a + n, n)


def kernel(
    slip_hbm, near_hbm, near_rows_hbm, near_cols_hbm, near_scale_hbm, left_hbm, right_hbm, far_rows_hbm, far_cols_hbm,
    far_rank_hbm, far_scale_hbm, depth_hbm, wet_hbm,
    both,
    slip, near_rows, near_cols, near_scale, far_rows, far_cols, far_rank, far_scale, depth, wet,
    slips, turned, near, left, right, coeffs, acc, chain, last, x_out, x_in, z_out, z_in, depths, compact, wets, strip_out, strip_in, east, north, h, e, n,
    load_sem, y_send, y_recv, x_send, x_recv, c_send, c_recv, k_send, k_recv, d_send, d_recv,
    p_send, p_recv, z_send, z_recv, h_send, h_recv,
):
    s, f = lax.axis_index("sea"), lax.axis_index("fault")
    y, x_lo, core = s // 4, (s // 2) % 2, s % 2
    z, x_hi = f // 2, f % 2
    core_mate, x_mate = s + 1 - 2 * core, s + 2 - 4 * x_lo
    far_mate = f + 1 - 2 * x_hi

    def copy(src, dst, send, recv, to_sea, to_fault):
        return pltpu.make_async_remote_copy(
            src_ref=src, dst_ref=dst, send_sem=send, recv_sem=recv, device_id=(to_sea, to_fault), device_id_type=MESH
        )

    barrier = pltpu.get_barrier_semaphore()
    partners = [(mod(s + 4 * d, SEA), f) for d in RING]
    partners += [(mod(x_mate + 4 * d, SEA), f) for d in DIRECT]
    partners += [(core_mate, f), (x_mate, f), (s, far_mate)]
    partners += [(s, mod(f + 2 * d, FAULT)) for d in RING]
    partners += [(mod(s + dy, SEA), mod(f + dx, FAULT)) for dy, dx in NEIGHBOURS]
    for partner in partners:
        pl.semaphore_signal(barrier, inc=1, device_id=partner, device_id_type=MESH)
    pairs = (
        (slip_hbm, slip), (depth_hbm, depth), (wet_hbm, wet), (near_rows_hbm, near_rows), (far_rows_hbm, far_rows),
        (near_cols_hbm, near_cols), (far_cols_hbm, far_cols), (far_rank_hbm, far_rank),
        (near_scale_hbm, near_scale), (far_scale_hbm, far_scale),
        (right_hbm.at[0, 0], right), (near_hbm.at[:, :, 0], near.at[0]), (near_hbm.at[:, :, 1], near.at[1]), (left_hbm.at[0, 0], left),
    )
    loads = [pltpu.make_async_copy(src, dst, load_sem.at[i]) for i, (src, dst) in enumerate(pairs)]
    for load in loads:
        load.start()
    for load in loads[:3]:
        load.wait()
    pl.semaphore_wait(barrier, len(partners))

    def slot(index):
        return slips.at[index // 2, pl.ds(pl.multiple_of((index % 2) * 128, 128), 128), :]

    def along_y(d, back):
        return copy(slip, slot(mod(s - 4 * d, SEA) if back else s), y_send.at[d], y_recv.at[d], mod(s + 4 * d, SEA), f)

    def to_mate(d, mate, send, recv, back):
        mine = mod(s - 4 * d, SEA)
        theirs = mod(mate - 4 * d, SEA)
        src = slip if d == 0 else slot(mine)
        return copy(src, slot(theirs if back else mine), send.at[d], recv.at[d], mate, f)

    def across(d):
        return copy(slip, slot(s), x_send.at[d], x_recv.at[d], mod(x_mate + 4 * d, SEA), f)

    def onward(d, back):
        mine = mod(x_mate - 4 * d, SEA)
        theirs = mod(s + 1 - 2 * core + 2 - 4 * x_lo - 4 * d, SEA)
        return copy(slot(mine), slot(theirs if back else mine), k_send.at[d], k_recv.at[d], core_mate, f)

    for d in RING:
        along_y(d, False).start()
        if d in DIRECT:
            across(d).start()
    to_mate(0, x_mate, x_send, x_recv, False).start()
    to_mate(0, core_mate, c_send, c_recv, False).start()
    slips[s // 2, pl.ds(pl.multiple_of((s % 2) * 128, 128), 128), :] = slip[...]

    wet_here = wet[...].astype(F32)
    depths[4] = jnp.zeros((BRICK, 128), F32)
    depths[4, :, :BRICK] = depth[...] * wet_here

    def depth_copy(i):
        dy, dx = NEIGHBOURS[i]
        k = (dy + 1) * 3 + dx + 1
        return copy(depths.at[4], depths.at[k], d_send.at[i], d_recv.at[i], mod(s - dy, SEA), mod(f - dx, FAULT))

    for i in range(8):
        depth_copy(i).start()

    acc[0] = jnp.zeros((2, LEAF // 2, MEMBERS), F32)
    for r in range(LEAVES):
        last[r] = 0

    def link(rows, first):
        def body(b, carry):
            row = rows[0, 0, b]
            chain[first + b] = last[row]
            for r in range(LEAVES):
                last[r] = jnp.where(row == r, first + b, last[r])
            return carry

        return body

    for load in loads[3:10]:
        load.wait()
    lax.fori_loop(0, NEAR, link(near_rows, 1), 0)
    lax.fori_loop(0, FAR, link(far_rows, 1 + NEAR), 0)

    def turn(g, carry):
        for i in range(8):
            b = 8 * g + i
            cells = left[b].T.reshape(8, 2, BRICK, RANK)
            for half in range(2):
                turned[b, half] = cells[:, half].reshape(LEAF // 2, RANK)
        return carry

    loads[13].wait()
    lax.fori_loop(0, FAR // 8, turn, 0)
    def ready(d):
        to_mate(d, x_mate, x_send, x_recv, True).wait_recv()
        onward(d, False).start()

    arrived = [0]
    for d in RING:
        along_y(d, True).wait_recv()
        if d not in DIRECT:
            to_mate(d, x_mate, x_send, x_recv, False).start()
        to_mate(d, core_mate, c_send, c_recv, False).start()
        arrived.append(d)
        if len(arrived) > LAG:
            ready(arrived.pop(0))
    for d in arrived:
        ready(d)

    for load in loads[10:13]:
        load.wait()
    for d in (0,) + RING:
        to_mate(d, core_mate, c_send, c_recv, True).wait_recv()
        onward(d, True).wait_recv()

    rank_of = lax.broadcasted_iota(jnp.int32, (RANK, MEMBERS), 0)

    def project(g, carry):
        for i in range(FAR_GROUP):
            b = g * FAR_GROUP + i
            made = jnp.dot(right[b], slips[far_cols[0, 0, b]], preferred_element_type=F32)
            coeffs[b] = jnp.where(rank_of < far_rank[0, 0, b], made, 0.0).astype(BF16)
        return carry

    def sums(half):
        for b in range(NEAR):
            block = near[half, b].reshape(LEAF // 2, LEAF)
            term = jnp.dot(block, slips[near_cols[0, 0, b]], preferred_element_type=F32)
            acc[1 + b, half] = term * near_scale[0, 0, b] + acc[chain[1 + b], half]
        for b in range(FAR):
            term = jnp.dot(turned[b, half], coeffs[b], preferred_element_type=F32)
            acc[1 + NEAR + b, half] = term * far_scale[0, 0, b] + acc[chain[1 + NEAR + b], half]

    lax.fori_loop(0, FAR // FAR_GROUP, project, 0)
    sums(1 - x_hi)

    def offset(j):
        return 4 + ((j + 1) // 2) * (1 - 2 * (j % 2))

    def part(j, half, r):
        place = pl.multiple_of(mod(z + offset(j), 8) * BRICK, BRICK)
        return acc[last[r], half, pl.ds(place, BRICK), :]

    def pair(j):
        return copy(x_out.at[j], x_in.at[j], p_send.at[j], p_recv.at[j], s, far_mate)

    def along_z(j):
        return copy(z_out.at[j], z_in.at[j], z_send.at[j], z_recv.at[j], s, 2 * mod(z + offset(j), 8) + x_hi)

    def send_pair(j, carry):
        for r in range(BRICK):
            x_out[j, r] = part(j, 1 - x_hi, r).astype(BF16)
        pair(j).start()
        return carry

    def send_z(j, carry):
        pair(j).wait_recv()
        for r in range(BRICK):
            z_out[j, r] = (part(j, x_hi, r) + x_in[j, r].astype(F32)).astype(BF16)
        along_z(j).start()
        return carry

    def geometry(j, carry):
        for i in range(4):
            edges(4 * j + i)
        for i in range(3):
            wets[3 * j + i] = spread(compact[1, pl.ds(3 * j + i, 1), :], BRICK)
        return carry

    def add_z(j, carry):
        along_z(j).wait_recv()
        for r in range(BRICK):
            both[0, r] = both[0, r] + z_in[j, r].astype(F32)
        return carry

    lax.fori_loop(0, 8, send_pair, 0)
    sums(x_hi)
    for i in range(8):
        depth_copy(i).wait_recv()
    lane = lax.broadcasted_iota(jnp.int32, (BRICK, 128), 1)
    west_ok, east_ok = f > 0, f < FAULT - 1
    for dy, place in ((-1, 0), (0, TOP), (1, TOP + BRICK)):
        row_ok = (s + dy >= 0) & (s + dy < SEA)
        k = (dy + 1) * 3
        west = jnp.where((lane >= 8) & (lane < 16) & west_ok, depths[k], 0.0)
        east_side = jnp.where((lane < 8) & east_ok, depths[k + 2], 0.0)
        band = pltpu.roll(west, 120, 1) + pltpu.roll(depths[k + 1], 8, 1) + pltpu.roll(east_side, 24, 1)
        band = jnp.where(row_ok, band, 0.0)
        rows = band[BRICK - STEPS :] if dy < 0 else band[:STEPS] if dy > 0 else band
        compact[0, place : place + rows.shape[0], :] = rows
    compact[0, ROWS:, :] = jnp.zeros((32 - ROWS, 128), F32)
    compact[1] = jnp.zeros((32, 128), F32)
    compact[1, :BRICK, :BRICK] = wet_here
    eye = lax.broadcasted_iota(jnp.int32, (COLS, 128), 1) == lax.broadcasted_iota(jnp.int32, (COLS, 128), 0)

    def spread(row, width):
        kept = jnp.where(eye[:width], jnp.broadcast_to(row, (width, 128)), 0.0)
        return jnp.broadcast_to(jnp.sum(kept, axis=1, keepdims=True), (width, 128))

    def edges(i):
        here = compact[0, pl.ds(i, 1), :]
        east[i] = spread(GAIN * jnp.minimum(here, pltpu.roll(here, 127, 1)), COLS)
        north[i] = spread(GAIN * jnp.minimum(here, compact[0, pl.ds(i + 1, 1), :]), COLS)

    lax.fori_loop(0, 7, send_z, 0)
    lax.fori_loop(0, 7, geometry, 0)
    pair(7).wait_recv()
    for r in range(BRICK):
        both[0, r] = part(7, x_hi, r) + x_in[7, r].astype(F32)
    lax.fori_loop(0, 7, add_z, 0)
    for r in range(BRICK):
        h[TOP + r, LEFT : LEFT + BRICK, :] = both[0, r] * wets[r]

    def span(i):
        dy, dx = NEIGHBOURS[i]
        tall, wide = (BRICK if dy == 0 else STEPS), (BRICK if dx == 0 else 8)
        src_y, dst_y = {-1: (TOP + BRICK - STEPS, 0), 0: (TOP, TOP), 1: (TOP, TOP + BRICK)}[dy]
        src_x, dst_x = {-1: (LEFT + BRICK - 8, 0), 0: (LEFT, LEFT), 1: (LEFT, LEFT + BRICK)}[dx]
        rows = 8 * tall
        src = (slice(src_y, src_y + tall), slice(src_x, src_x + wide), slice(None))
        dst = (slice(dst_y, dst_y + tall), slice(dst_x, dst_x + wide), slice(None))
        return dx, rows, src, dst

    def halo(i):
        dy, dx = NEIGHBOURS[i]
        _, rows, src, dst = span(i)
        to_sea, to_fault = mod(s - dy, SEA), mod(f - dx, FAULT)
        if dx == 0:
            return copy(h.at[src], h.at[dst], h_send.at[i], h_recv.at[i], to_sea, to_fault)
        return copy(strip_out.at[i, :rows], strip_in.at[i, :rows], h_send.at[i], h_recv.at[i], to_sea, to_fault)

    for i in range(8):
        dx, rows, src, _ = span(i)
        if dx:
            strip_out[i, :rows] = h[src].reshape(rows, MEMBERS).astype(BF16)
        halo(i).start()
    e[...] = jnp.zeros(e.shape, F32)
    n[...] = jnp.zeros(n.shape, F32)
    for d in RING:
        along_y(d, False).wait_send()
    for d in (0,) + RING:
        to_mate(d, x_mate, x_send, x_recv, False).wait_send()
        to_mate(d, core_mate, c_send, c_recv, False).wait_send()
        onward(d, False).wait_send()
    for i in range(8):
        depth_copy(i).wait_send()
    for j in range(8):
        pair(j).wait_send()
    for j in range(7):
        along_z(j).wait_send()
    for i in range(8):
        dx, rows, _, dst = span(i)
        halo(i).wait()
        if dx:
            h[dst] = strip_in[i, :rows].astype(F32).reshape(rows // 8, 8, MEMBERS)

    for step in range(STEPS):
        def rows(i, count, below):
            here = [h[i + k] for k in range(count + 1)]
            flows = [n[i + k] + (here[k + 1] - here[k]) for k in range(count)]
            eastward = [e[i + k] + (pltpu.roll(here[k], COLS - 1, 0) - here[k]) for k in range(count)]
            fluxes = [below] + [north[i + k] * flows[k] for k in range(count)]
            sideways = [east[i + k] * eastward[k] for k in range(count)]
            change = [side - pltpu.roll(side, 1, 0) for side in sideways]
            for k in range(count):
                n[i + k] = flows[k]
                e[i + k] = eastward[k]
                h[i + k] = here[k] + (change[k] + (fluxes[k + 1] - fluxes[k]))
            return fluxes[-1]

        count = ROWS - 2 - 2 * step
        flow = n[step] + (h[step + 1] - h[step])
        n[step] = flow
        below = north[step] * flow
        below = lax.fori_loop(0, count // TALL, lambda g, carry: rows(step + 1 + TALL * g, TALL, carry), below)
        if count % TALL:
            rows(ROWS - 1 - step - count % TALL, count % TALL, below)
    both[1] = h[TOP : TOP + BRICK, LEFT : LEFT + BRICK, :]


def on_device(*args):
    hbm = pl.BlockSpec(memory_space=pltpu.HBM)
    field = pltpu.VMEM((ROWS, COLS, MEMBERS), F32)
    dma = pltpu.SemaphoreType.DMA
    brick = jax.ShapeDtypeStruct((BRICK, BRICK, MEMBERS), F32)
    near = args[1].reshape(NEAR, 8, 2, BRICK, LEAF)
    made = pl.pallas_call(
        kernel,
        out_shape=pltpu.VMEM((2, BRICK, BRICK, MEMBERS), F32),
        in_specs=[hbm] * 13,
        out_specs=pl.BlockSpec(memory_space=pltpu.VMEM),
        scratch_shapes=[
            pltpu.VMEM((128, MEMBERS), BF16),
            *(pltpu.SMEM((1, 1, NEAR), kind) for kind in (jnp.int32, jnp.int32, F32)),
            *(pltpu.SMEM((1, 1, FAR), kind) for kind in (jnp.int32, jnp.int32, jnp.int32, F32)),
            pltpu.VMEM((BRICK, BRICK), F32),
            pltpu.VMEM((BRICK, BRICK), jnp.int32),
            pltpu.VMEM((LEAVES, LEAF, MEMBERS), BF16),
            pltpu.VMEM((FAR, 2, LEAF // 2, RANK), BF16),
            pltpu.VMEM((2, NEAR, 8, BRICK, LEAF), BF16),
            pltpu.VMEM((FAR, RANK, LEAF), BF16),
            pltpu.VMEM((FAR, RANK, LEAF), BF16),
            pltpu.VMEM((FAR, RANK, MEMBERS), BF16),
            pltpu.VMEM((1 + NEAR + FAR, 2, LEAF // 2, MEMBERS), F32),
            pltpu.SMEM((1 + NEAR + FAR,), jnp.int32),
            pltpu.SMEM((LEAVES,), jnp.int32),
            pltpu.VMEM((8, BRICK, BRICK, MEMBERS), BF16),
            pltpu.VMEM((8, BRICK, BRICK, MEMBERS), BF16),
            pltpu.VMEM((7, BRICK, BRICK, MEMBERS), BF16),
            pltpu.VMEM((7, BRICK, BRICK, MEMBERS), BF16),
            pltpu.VMEM((9, BRICK, 128), F32),
            pltpu.VMEM((2, 32, 128), F32),
            pltpu.VMEM((21, BRICK, MEMBERS), F32),
            pltpu.VMEM((8, 8 * BRICK, MEMBERS), BF16), pltpu.VMEM((8, 8 * BRICK, MEMBERS), BF16),
            field, field, field, field, field,
            dma((14,)),
            dma((8,)), dma((8,)), dma((8,)), dma((8,)), dma((8,)), dma((8,)), dma((8,)), dma((8,)),
            dma((8,)), dma((8,)),
            dma((8,)), dma((8,)), dma((7,)), dma((7,)), dma((8,)), dma((8,)),
        ],
        compiler_params=pltpu.CompilerParams(
            collective_id=0, has_side_effects=True, vmem_limit_bytes=62 * 2**20
        ),
        name="forecast",
    )(args[0], near, *args[2:])
    return made[0], made[1]


def solution(mesh):
    blocks = P("sea", "fault", None, None, None)
    lists = P("sea", "fault", None)
    cells = P("sea", "fault")
    return jax.shard_map(
        on_device,
        mesh=mesh,
        in_specs=(
            P(("fault", "sea"), None), blocks, lists, lists, lists, blocks, blocks, lists, lists, lists, lists, cells, cells,
        ),
        out_specs=(lists, lists),
        check_vma=False,
    )
```

```python
import jax
import jax.numpy as jnp
from jax import lax
from jax.experimental import pallas as pl
from jax.experimental.pallas import tpu as pltpu
from jax.sharding import PartitionSpec as P

STEPS = 6
GRAVITY_STEP = 0.7
HEIGHT_STEP = 0.7
GAIN = GRAVITY_STEP * HEIGHT_STEP
MESH = pl.DeviceIdType.MESH
F32, BF16 = jnp.float32, jnp.bfloat16

SEA, FAULT = 32, 16
LEAF, MEMBERS, RANK = 256, 128, 48
NEAR, FAR, LEAVES = 8, 24, 16
BRICK = 16
ROWS, COLS = BRICK + 2 * STEPS, BRICK + 16
TOP, LEFT = STEPS, 8
NEIGHBOURS = [(-1, 0), (1, 0), (-1, -1), (-1, 1), (1, -1), (1, 1), (0, -1), (0, 1)]
RING = (1, 7, 2, 6, 3, 5, 4)
TALL = 4
FAR_GROUP = 24
DIRECT = (4,)
LAG = 4


def mod(a, n):
    return lax.rem(a + n, n)


def kernel(
    slip_hbm, near_hbm, near_rows_hbm, near_cols_hbm, near_scale_hbm, left_hbm, right_hbm, far_rows_hbm, far_cols_hbm,
    far_rank_hbm, far_scale_hbm, depth_hbm, wet_hbm,
    both,
    slip, near_rows, near_cols, near_scale, far_rows, far_cols, far_rank, far_scale, depth, wet,
    slips, turned, near, left, right, coeffs, acc, chain, last, x_out, x_in, z_out, z_in, depths, compact, wets, strip_out, strip_in, east, north, h, e, n,
    load_sem, y_send, y_recv, x_send, x_recv, c_send, c_recv, k_send, k_recv, d_send, d_recv,
    p_send, p_recv, z_send, z_recv, h_send, h_recv,
):
    s, f = lax.axis_index("sea"), lax.axis_index("fault")
    y, x_lo, core = s // 4, (s // 2) % 2, s % 2
    z, x_hi = f // 2, f % 2
    core_mate, x_mate = s + 1 - 2 * core, s + 2 - 4 * x_lo
    far_mate = f + 1 - 2 * x_hi

    def copy(src, dst, send, recv, to_sea, to_fault):
        return pltpu.make_async_remote_copy(
            src_ref=src, dst_ref=dst, send_sem=send, recv_sem=recv, device_id=(to_sea, to_fault), device_id_type=MESH
        )

    barrier = pltpu.get_barrier_semaphore()
    partners = [(mod(s + 4 * d, SEA), f) for d in RING]
    partners += [(mod(x_mate + 4 * d, SEA), f) for d in DIRECT]
    partners += [(core_mate, f), (x_mate, f), (s, far_mate)]
    partners += [(s, mod(f + 2 * d, FAULT)) for d in RING]
    partners += [(mod(s + dy, SEA), mod(f + dx, FAULT)) for dy, dx in NEIGHBOURS]
    for partner in partners:
        pl.semaphore_signal(barrier, inc=1, device_id=partner, device_id_type=MESH)
    pairs = (
        (slip_hbm, slip), (depth_hbm, depth), (wet_hbm, wet), (near_rows_hbm, near_rows), (far_rows_hbm, far_rows),
        (near_cols_hbm, near_cols), (far_cols_hbm, far_cols), (far_rank_hbm, far_rank),
        (near_scale_hbm, near_scale), (far_scale_hbm, far_scale),
        (right_hbm.at[0, 0], right), (near_hbm.at[:, :, 0], near.at[0]), (near_hbm.at[:, :, 1], near.at[1]), (left_hbm.at[0, 0], left),
    )
    loads = [pltpu.make_async_copy(src, dst, load_sem.at[i]) for i, (src, dst) in enumerate(pairs)]
    for load in loads:
        load.start()
    for load in loads[:3]:
        load.wait()
    pl.semaphore_wait(barrier, len(partners))

    def slot(index):
        return slips.at[index // 2, pl.ds(pl.multiple_of((index % 2) * 128, 128), 128), :]

    def along_y(d, back):
        return copy(slip, slot(mod(s - 4 * d, SEA) if back else s), y_send.at[d], y_recv.at[d], mod(s + 4 * d, SEA), f)

    def to_mate(d, mate, send, recv, back):
        mine = mod(s - 4 * d, SEA)
        theirs = mod(mate - 4 * d, SEA)
        src = slip if d == 0 else slot(mine)
        return copy(src, slot(theirs if back else mine), send.at[d], recv.at[d], mate, f)

    def across(d):
        return copy(slip, slot(s), x_send.at[d], x_recv.at[d], mod(x_mate + 4 * d, SEA), f)

    def onward(d, back):
        mine = mod(x_mate - 4 * d, SEA)
        theirs = mod(s + 1 - 2 * core + 2 - 4 * x_lo - 4 * d, SEA)
        return copy(slot(mine), slot(theirs if back else mine), k_send.at[d], k_recv.at[d], core_mate, f)

    for d in RING:
        along_y(d, False).start()
        if d in DIRECT:
            across(d).start()
    to_mate(0, x_mate, x_send, x_recv, False).start()
    to_mate(0, core_mate, c_send, c_recv, False).start()
    slips[s // 2, pl.ds(pl.multiple_of((s % 2) * 128, 128), 128), :] = slip[...]

    wet_here = wet[...].astype(F32)
    depths[4] = jnp.zeros((BRICK, 128), F32)
    depths[4, :, :BRICK] = depth[...] * wet_here

    def depth_copy(i):
        dy, dx = NEIGHBOURS[i]
        k = (dy + 1) * 3 + dx + 1
        return copy(depths.at[4], depths.at[k], d_send.at[i], d_recv.at[i], mod(s - dy, SEA), mod(f - dx, FAULT))

    for i in range(8):
        depth_copy(i).start()

    acc[0] = jnp.zeros((2, LEAF // 2, MEMBERS), F32)
    for r in range(LEAVES):
        last[r] = 0

    def link(rows, first):
        def body(b, carry):
            row = rows[0, 0, b]
            chain[first + b] = last[row]
            for r in range(LEAVES):
                last[r] = jnp.where(row == r, first + b, last[r])
            return carry

        return body

    for load in loads[3:10]:
        load.wait()
    lax.fori_loop(0, NEAR, link(near_rows, 1), 0)
    lax.fori_loop(0, FAR, link(far_rows, 1 + NEAR), 0)

    def turn(g, carry):
        for i in range(8):
            b = 8 * g + i
            cells = left[b].T.reshape(8, 2, BRICK, RANK)
            for half in range(2):
                turned[b, half] = cells[:, half].reshape(LEAF // 2, RANK)
        return carry

    loads[13].wait()
    lax.fori_loop(0, FAR // 8, turn, 0)
    def ready(d):
        to_mate(d, x_mate, x_send, x_recv, True).wait_recv()
        onward(d, False).start()

    arrived = [0]
    for d in RING:
        along_y(d, True).wait_recv()
        if d not in DIRECT:
            to_mate(d, x_mate, x_send, x_recv, False).start()
        to_mate(d, core_mate, c_send, c_recv, False).start()
        arrived.append(d)
        if len(arrived) > LAG:
            ready(arrived.pop(0))
    for d in arrived:
        ready(d)

    for load in loads[10:13]:
        load.wait()
    for d in (0,) + RING:
        to_mate(d, core_mate, c_send, c_recv, True).wait_recv()
        onward(d, True).wait_recv()

    rank_of = lax.broadcasted_iota(jnp.int32, (RANK, MEMBERS), 0)

    def project(g, carry):
        for i in range(FAR_GROUP):
            b = g * FAR_GROUP + i
            made = jnp.dot(right[b], slips[far_cols[0, 0, b]], preferred_element_type=F32)
            coeffs[b] = jnp.where(rank_of < far_rank[0, 0, b], made, 0.0).astype(BF16)
        return carry

    def sums(half):
        for b in range(NEAR):
            block = near[half, b].reshape(LEAF // 2, LEAF)
            term = jnp.dot(block, slips[near_cols[0, 0, b]], preferred_element_type=F32)
            acc[1 + b, half] = term * near_scale[0, 0, b] + acc[chain[1 + b], half]
        for b in range(FAR):
            term = jnp.dot(turned[b, half], coeffs[b], preferred_element_type=F32)
            acc[1 + NEAR + b, half] = term * far_scale[0, 0, b] + acc[chain[1 + NEAR + b], half]

    lax.fori_loop(0, FAR // FAR_GROUP, project, 0)
    sums(1 - x_hi)

    def offset(j):
        return 4 + ((j + 1) // 2) * (1 - 2 * (j % 2))

    def part(j, half, r):
        place = pl.multiple_of(mod(z + offset(j), 8) * BRICK, BRICK)
        return acc[last[r], half, pl.ds(place, BRICK), :]

    def pair(j):
        return copy(x_out.at[j], x_in.at[j], p_send.at[j], p_recv.at[j], s, far_mate)

    def along_z(j):
        return copy(z_out.at[j], z_in.at[j], z_send.at[j], z_recv.at[j], s, 2 * mod(z + offset(j), 8) + x_hi)

    def send_pair(j, carry):
        for r in range(BRICK):
            x_out[j, r] = part(j, 1 - x_hi, r).astype(BF16)
        pair(j).start()
        return carry

    def send_z(j, carry):
        pair(j).wait_recv()
        for r in range(BRICK):
            z_out[j, r] = (part(j, x_hi, r) + x_in[j, r].astype(F32)).astype(BF16)
        along_z(j).start()
        return carry

    def geometry(j, carry):
        for i in range(4):
            edges(4 * j + i)
        for i in range(3):
            wets[3 * j + i] = spread(compact[1, pl.ds(3 * j + i, 1), :], BRICK)
        return carry

    def add_z(j, carry):
        along_z(j).wait_recv()
        for r in range(BRICK):
            both[0, r] = both[0, r] + z_in[j, r].astype(F32)
        return carry

    lax.fori_loop(0, 8, send_pair, 0)
    sums(x_hi)
    for i in range(8):
        depth_copy(i).wait_recv()
    lane = lax.broadcasted_iota(jnp.int32, (BRICK, 128), 1)
    west_ok, east_ok = f > 0, f < FAULT - 1
    for dy, place in ((-1, 0), (0, TOP), (1, TOP + BRICK)):
        row_ok = (s + dy >= 0) & (s + dy < SEA)
        k = (dy + 1) * 3
        west = jnp.where((lane >= 8) & (lane < 16) & west_ok, depths[k], 0.0)
        east_side = jnp.where((lane < 8) & east_ok, depths[k + 2], 0.0)
        band = pltpu.roll(west, 120, 1) + pltpu.roll(depths[k + 1], 8, 1) + pltpu.roll(east_side, 24, 1)
        band = jnp.where(row_ok, band, 0.0)
        rows = band[BRICK - STEPS :] if dy < 0 else band[:STEPS] if dy > 0 else band
        compact[0, place : place + rows.shape[0], :] = rows
    compact[0, ROWS:, :] = jnp.zeros((32 - ROWS, 128), F32)
    compact[1] = jnp.zeros((32, 128), F32)
    compact[1, :BRICK, :BRICK] = wet_here
    eye = lax.broadcasted_iota(jnp.int32, (COLS, 128), 1) == lax.broadcasted_iota(jnp.int32, (COLS, 128), 0)

    def spread(row, width):
        kept = jnp.where(eye[:width], jnp.broadcast_to(row, (width, 128)), 0.0)
        return jnp.broadcast_to(jnp.sum(kept, axis=1, keepdims=True), (width, 128))

    def edges(i):
        here = compact[0, pl.ds(i, 1), :]
        east[i] = spread(GAIN * jnp.minimum(here, pltpu.roll(here, 127, 1)), COLS)
        north[i] = spread(GAIN * jnp.minimum(here, compact[0, pl.ds(i + 1, 1), :]), COLS)

    lax.fori_loop(0, 7, send_z, 0)
    lax.fori_loop(0, 7, geometry, 0)
    pair(7).wait_recv()
    for r in range(BRICK):
        both[0, r] = part(7, x_hi, r) + x_in[7, r].astype(F32)
    lax.fori_loop(0, 7, add_z, 0)
    for r in range(BRICK):
        h[TOP + r, LEFT : LEFT + BRICK, :] = both[0, r] * wets[r]

    def span(i):
        dy, dx = NEIGHBOURS[i]
        tall, wide = (BRICK if dy == 0 else STEPS), (BRICK if dx == 0 else 8)
        src_y, dst_y = {-1: (TOP + BRICK - STEPS, 0), 0: (TOP, TOP), 1: (TOP, TOP + BRICK)}[dy]
        src_x, dst_x = {-1: (LEFT + BRICK - 8, 0), 0: (LEFT, LEFT), 1: (LEFT, LEFT + BRICK)}[dx]
        rows = 8 * tall
        src = (slice(src_y, src_y + tall), slice(src_x, src_x + wide), slice(None))
        dst = (slice(dst_y, dst_y + tall), slice(dst_x, dst_x + wide), slice(None))
        return dx, rows, src, dst

    def halo(i):
        dy, dx = NEIGHBOURS[i]
        _, rows, src, dst = span(i)
        to_sea, to_fault = mod(s - dy, SEA), mod(f - dx, FAULT)
        if dx == 0:
            return copy(h.at[src], h.at[dst], h_send.at[i], h_recv.at[i], to_sea, to_fault)
        return copy(strip_out.at[i, :rows], strip_in.at[i, :rows], h_send.at[i], h_recv.at[i], to_sea, to_fault)

    for i in range(8):
        dx, rows, src, _ = span(i)
        if dx:
            strip_out[i, :rows] = h[src].reshape(rows, MEMBERS).astype(BF16)
        halo(i).start()
    e[...] = jnp.zeros(e.shape, F32)
    n[...] = jnp.zeros(n.shape, F32)
    for d in RING:
        along_y(d, False).wait_send()
    for d in (0,) + RING:
        to_mate(d, x_mate, x_send, x_recv, False).wait_send()
        to_mate(d, core_mate, c_send, c_recv, False).wait_send()
        onward(d, False).wait_send()
    for i in range(8):
        depth_copy(i).wait_send()
    for j in range(8):
        pair(j).wait_send()
    for j in range(7):
        along_z(j).wait_send()
    for i in range(8):
        dx, rows, _, dst = span(i)
        halo(i).wait()
        if dx:
            h[dst] = strip_in[i, :rows].astype(F32).reshape(rows // 8, 8, MEMBERS)

    for step in range(STEPS):
        def rows(i, count, below):
            here = [h[i + k] for k in range(count + 1)]
            flows = [n[i + k] + (here[k + 1] - here[k]) for k in range(count)]
            eastward = [e[i + k] + (pltpu.roll(here[k], COLS - 1, 0) - here[k]) for k in range(count)]
            fluxes = [below] + [north[i + k] * flows[k] for k in range(count)]
            sideways = [east[i + k] * eastward[k] for k in range(count)]
            change = [side - pltpu.roll(side, 1, 0) for side in sideways]
            for k in range(count):
                n[i + k] = flows[k]
                e[i + k] = eastward[k]
                h[i + k] = here[k] + (change[k] + (fluxes[k + 1] - fluxes[k]))
            return fluxes[-1]

        count = ROWS - 2 - 2 * step
        flow = n[step] + (h[step + 1] - h[step])
        n[step] = flow
        below = north[step] * flow
        below = lax.fori_loop(0, count // TALL, lambda g, carry: rows(step + 1 + TALL * g, TALL, carry), below)
        if count % TALL:
            rows(ROWS - 1 - step - count % TALL, count % TALL, below)
    both[1] = h[TOP : TOP + BRICK, LEFT : LEFT + BRICK, :]


def on_device(*args):
    hbm = pl.BlockSpec(memory_space=pltpu.HBM)
    field = pltpu.VMEM((ROWS, COLS, MEMBERS), F32)
    dma = pltpu.SemaphoreType.DMA
    brick = jax.ShapeDtypeStruct((BRICK, BRICK, MEMBERS), F32)
    near = args[1].reshape(NEAR, 8, 2, BRICK, LEAF)
    made = pl.pallas_call(
        kernel,
        out_shape=pltpu.VMEM((2, BRICK, BRICK, MEMBERS), F32),
        in_specs=[hbm] * 13,
        out_specs=pl.BlockSpec(memory_space=pltpu.VMEM),
        scratch_shapes=[
            pltpu.VMEM((128, MEMBERS), BF16),
            *(pltpu.SMEM((1, 1, NEAR), kind) for kind in (jnp.int32, jnp.int32, F32)),
            *(pltpu.SMEM((1, 1, FAR), kind) for kind in (jnp.int32, jnp.int32, jnp.int32, F32)),
            pltpu.VMEM((BRICK, BRICK), F32),
            pltpu.VMEM((BRICK, BRICK), jnp.int32),
            pltpu.VMEM((LEAVES, LEAF, MEMBERS), BF16),
            pltpu.VMEM((FAR, 2, LEAF // 2, RANK), BF16),
            pltpu.VMEM((2, NEAR, 8, BRICK, LEAF), BF16),
            pltpu.VMEM((FAR, RANK, LEAF), BF16),
            pltpu.VMEM((FAR, RANK, LEAF), BF16),
            pltpu.VMEM((FAR, RANK, MEMBERS), BF16),
            pltpu.VMEM((1 + NEAR + FAR, 2, LEAF // 2, MEMBERS), F32),
            pltpu.SMEM((1 + NEAR + FAR,), jnp.int32),
            pltpu.SMEM((LEAVES,), jnp.int32),
            pltpu.VMEM((8, BRICK, BRICK, MEMBERS), BF16),
            pltpu.VMEM((8, BRICK, BRICK, MEMBERS), BF16),
            pltpu.VMEM((7, BRICK, BRICK, MEMBERS), BF16),
            pltpu.VMEM((7, BRICK, BRICK, MEMBERS), BF16),
            pltpu.VMEM((9, BRICK, 128), F32),
            pltpu.VMEM((2, 32, 128), F32),
            pltpu.VMEM((21, BRICK, MEMBERS), F32),
            pltpu.VMEM((8, 8 * BRICK, MEMBERS), BF16), pltpu.VMEM((8, 8 * BRICK, MEMBERS), BF16),
            field, field, field, field, field,
            dma((14,)),
            dma((8,)), dma((8,)), dma((8,)), dma((8,)), dma((8,)), dma((8,)), dma((8,)), dma((8,)),
            dma((8,)), dma((8,)),
            dma((8,)), dma((8,)), dma((7,)), dma((7,)), dma((8,)), dma((8,)),
        ],
        compiler_params=pltpu.CompilerParams(
            collective_id=0, has_side_effects=True, vmem_limit_bytes=62 * 2**20
        ),
        name="forecast",
    )(args[0], near, *args[2:])
    return made[0], made[1]


def solution(mesh):
    blocks = P("sea", "fault", None, None, None)
    lists = P("sea", "fault", None)
    cells = P("sea", "fault")
    return jax.shard_map(
        on_device,
        mesh=mesh,
        in_specs=(
            P(("fault", "sea"), None), blocks, lists, lists, lists, blocks, blocks, lists, lists, lists, lists, cells, cells,
        ),
        out_specs=(lists, lists),
        check_vma=False,
    )
```

```python
import jax
import jax.numpy as jnp
from jax import lax
from jax.experimental import pallas as pl
from jax.experimental.pallas import tpu as pltpu
from jax.sharding import PartitionSpec as P

STEPS = 6
GRAVITY_STEP = 0.7
HEIGHT_STEP = 0.7
GAIN = GRAVITY_STEP * HEIGHT_STEP
MESH = pl.DeviceIdType.MESH
F32, BF16 = jnp.float32, jnp.bfloat16

SEA, FAULT = 32, 16
LEAF, MEMBERS, RANK = 256, 128, 48
NEAR, FAR, LEAVES = 8, 24, 16
BRICK = 16
ROWS, COLS = BRICK + 2 * STEPS, BRICK + 16
TOP, LEFT = STEPS, 8
NEIGHBOURS = [(-1, 0), (1, 0), (-1, -1), (-1, 1), (1, -1), (1, 1), (0, -1), (0, 1)]
RING = (1, 7, 2, 6, 3, 5, 4)
TALL = 4
FAR_GROUP = 24
DIRECT = (4,)
LAG = 4


def mod(a, n):
    return lax.rem(a + n, n)


def kernel(
    slip_hbm, near_hbm, near_rows_hbm, near_cols_hbm, near_scale_hbm, left_hbm, right_hbm, far_rows_hbm, far_cols_hbm,
    far_rank_hbm, far_scale_hbm, depth_hbm, wet_hbm,
    both,
    slip, near_rows, near_cols, near_scale, far_rows, far_cols, far_rank, far_scale, depth, wet,
    slips, turned, near, left, right, coeffs, acc, chain, last, x_out, x_in, z_out, z_in, depths, compact, wets, strip_out, strip_in, east, north, h, e, n,
    load_sem, y_send, y_recv, x_send, x_recv, c_send, c_recv, k_send, k_recv, d_send, d_recv,
    p_send, p_recv, z_send, z_recv, h_send, h_recv,
):
    s, f = lax.axis_index("sea"), lax.axis_index("fault")
    y, x_lo, core = s // 4, (s // 2) % 2, s % 2
    z, x_hi = f // 2, f % 2
    core_mate, x_mate = s + 1 - 2 * core, s + 2 - 4 * x_lo
    far_mate = f + 1 - 2 * x_hi

    def copy(src, dst, send, recv, to_sea, to_fault):
        return pltpu.make_async_remote_copy(
            src_ref=src, dst_ref=dst, send_sem=send, recv_sem=recv, device_id=(to_sea, to_fault), device_id_type=MESH
        )

    barrier = pltpu.get_barrier_semaphore()
    partners = [(mod(s + 4 * d, SEA), f) for d in RING]
    partners += [(mod(x_mate + 4 * d, SEA), f) for d in DIRECT]
    partners += [(core_mate, f), (x_mate, f), (s, far_mate)]
    partners += [(s, mod(f + 2 * d, FAULT)) for d in RING]
    partners += [(mod(s + dy, SEA), mod(f + dx, FAULT)) for dy, dx in NEIGHBOURS]
    for partner in partners:
        pl.semaphore_signal(barrier, inc=1, device_id=partner, device_id_type=MESH)
    pairs = (
        (slip_hbm, slip), (depth_hbm, depth), (wet_hbm, wet), (near_rows_hbm, near_rows), (far_rows_hbm, far_rows),
        (near_cols_hbm, near_cols), (far_cols_hbm, far_cols), (far_rank_hbm, far_rank),
        (near_scale_hbm, near_scale), (far_scale_hbm, far_scale),
        (right_hbm.at[0, 0], right), (near_hbm.at[:, :, 0], near.at[0]), (near_hbm.at[:, :, 1], near.at[1]), (left_hbm.at[0, 0], left),
    )
    loads = [pltpu.make_async_copy(src, dst, load_sem.at[i]) for i, (src, dst) in enumerate(pairs)]
    for load in loads:
        load.start()
    for load in loads[:3]:
        load.wait()
    pl.semaphore_wait(barrier, len(partners))

    def slot(index):
        return slips.at[index // 2, pl.ds(pl.multiple_of((index % 2) * 128, 128), 128), :]

    def along_y(d, back):
        return copy(slip, slot(mod(s - 4 * d, SEA) if back else s), y_send.at[d], y_recv.at[d], mod(s + 4 * d, SEA), f)

    def to_mate(d, mate, send, recv, back):
        mine = mod(s - 4 * d, SEA)
        theirs = mod(mate - 4 * d, SEA)
        src = slip if d == 0 else slot(mine)
        return copy(src, slot(theirs if back else mine), send.at[d], recv.at[d], mate, f)

    def across(d):
        return copy(slip, slot(s), x_send.at[d], x_recv.at[d], mod(x_mate + 4 * d, SEA), f)

    def onward(d, back):
        mine = mod(x_mate - 4 * d, SEA)
        theirs = mod(s + 1 - 2 * core + 2 - 4 * x_lo - 4 * d, SEA)
        return copy(slot(mine), slot(theirs if back else mine), k_send.at[d], k_recv.at[d], core_mate, f)

    for d in RING:
        along_y(d, False).start()
        if d in DIRECT:
            across(d).start()
    to_mate(0, x_mate, x_send, x_recv, False).start()
    to_mate(0, core_mate, c_send, c_recv, False).start()
    slips[s // 2, pl.ds(pl.multiple_of((s % 2) * 128, 128), 128), :] = slip[...]

    wet_here = wet[...].astype(F32)
    depths[4] = jnp.zeros((BRICK, 128), F32)
    depths[4, :, :BRICK] = depth[...] * wet_here

    def depth_copy(i):
        dy, dx = NEIGHBOURS[i]
        k = (dy + 1) * 3 + dx + 1
        return copy(depths.at[4], depths.at[k], d_send.at[i], d_recv.at[i], mod(s - dy, SEA), mod(f - dx, FAULT))

    for i in range(8):
        depth_copy(i).start()

    acc[0] = jnp.zeros((2, LEAF // 2, MEMBERS), F32)
    for r in range(LEAVES):
        last[r] = 0

    def link(rows, first):
        def body(b, carry):
            row = rows[0, 0, b]
            chain[first + b] = last[row]
            for r in range(LEAVES):
                last[r] = jnp.where(row == r, first + b, last[r])
            return carry

        return body

    for load in loads[3:10]:
        load.wait()
    lax.fori_loop(0, NEAR, link(near_rows, 1), 0)
    lax.fori_loop(0, FAR, link(far_rows, 1 + NEAR), 0)

    def turn(g, carry):
        for i in range(8):
            b = 8 * g + i
            cells = left[b].T.reshape(8, 2, BRICK, RANK)
            for half in range(2):
                turned[b, half] = cells[:, half].reshape(LEAF // 2, RANK)
        return carry

    loads[13].wait()
    lax.fori_loop(0, FAR // 8, turn, 0)
    def ready(d):
        to_mate(d, x_mate, x_send, x_recv, True).wait_recv()
        onward(d, False).start()

    arrived = [0]
    for d in RING:
        along_y(d, True).wait_recv()
        if d not in DIRECT:
            to_mate(d, x_mate, x_send, x_recv, False).start()
        to_mate(d, core_mate, c_send, c_recv, False).start()
        arrived.append(d)
        if len(arrived) > LAG:
            ready(arrived.pop(0))
    for d in arrived:
        ready(d)

    for load in loads[10:13]:
        load.wait()
    for d in (0,) + RING:
        to_mate(d, core_mate, c_send, c_recv, True).wait_recv()
        onward(d, True).wait_recv()

    rank_of = lax.broadcasted_iota(jnp.int32, (RANK, MEMBERS), 0)

    def project(g, carry):
        for i in range(FAR_GROUP):
            b = g * FAR_GROUP + i
            made = jnp.dot(right[b], slips[far_cols[0, 0, b]], preferred_element_type=F32)
            coeffs[b] = jnp.where(rank_of < far_rank[0, 0, b], made, 0.0).astype(BF16)
        return carry

    def sums(half):
        for b in range(NEAR):
            block = near[half, b].reshape(LEAF // 2, LEAF)
            term = jnp.dot(block, slips[near_cols[0, 0, b]], preferred_element_type=F32)
            acc[1 + b, half] = term * near_scale[0, 0, b] + acc[chain[1 + b], half]
        for b in range(FAR):
            term = jnp.dot(turned[b, half], coeffs[b], preferred_element_type=F32)
            acc[1 + NEAR + b, half] = term * far_scale[0, 0, b] + acc[chain[1 + NEAR + b], half]

    lax.fori_loop(0, FAR // FAR_GROUP, project, 0)
    sums(1 - x_hi)

    def offset(j):
        k = (j + 1) // 2
        return 4 + (k + ((k // 2) % 2) * (5 - 2 * k)) * (1 - 2 * (j % 2))

    def relay(half):
        rows = slice(8 * half, 8 * half + 8)
        to_fault = 2 * mod(z + (2 if half else 6), 8) + x_hi
        return copy(z_out.at[0, rows], z_in.at[0, rows], z_send.at[7 * half], z_recv.at[7 * half], s, to_fault)

    def part(j, half, r):
        place = pl.multiple_of(mod(z + offset(j), 8) * BRICK, BRICK)
        return acc[last[r], half, pl.ds(place, BRICK), :]

    def pair(j):
        return copy(x_out.at[j], x_in.at[j], p_send.at[j], p_recv.at[j], s, far_mate)

    def along_z(j):
        return copy(z_out.at[j], z_in.at[j], z_send.at[j], z_recv.at[j], s, 2 * mod(z + offset(j), 8) + x_hi)

    def send_pair(j, carry):
        for r in range(BRICK):
            x_out[j, r] = part(j, 1 - x_hi, r).astype(BF16)
        pair(j).start()
        return carry

    def pair_sum(j, extra):
        pair(j).wait_recv()
        for r in range(BRICK):
            both_sides = part(j, x_hi, r) + x_in[j, r].astype(F32)
            if r in extra:
                both_sides = both_sides + z_in[0, r].astype(F32)
            z_out[j, r] = both_sides.astype(BF16)

    def send_z(j, carry):
        pair_sum(j, ())
        along_z(j).start()
        return carry

    def geometry(j, carry):
        for i in range(4):
            edges(4 * j + i)
        for i in range(3):
            wets[3 * j + i] = spread(compact[1, pl.ds(3 * j + i, 1), :], BRICK)
        return carry

    def add_z(j, carry):
        along_z(j).wait_recv()
        for r in range(BRICK):
            both[0, r] = both[0, r] + z_in[j, r].astype(F32)
        return carry

    lax.fori_loop(0, 8, send_pair, 0)
    sums(x_hi)
    for i in range(8):
        depth_copy(i).wait_recv()
    lane = lax.broadcasted_iota(jnp.int32, (BRICK, 128), 1)
    west_ok, east_ok = f > 0, f < FAULT - 1
    for dy, place in ((-1, 0), (0, TOP), (1, TOP + BRICK)):
        row_ok = (s + dy >= 0) & (s + dy < SEA)
        k = (dy + 1) * 3
        west = jnp.where((lane >= 8) & (lane < 16) & west_ok, depths[k], 0.0)
        east_side = jnp.where((lane < 8) & east_ok, depths[k + 2], 0.0)
        band = pltpu.roll(west, 120, 1) + pltpu.roll(depths[k + 1], 8, 1) + pltpu.roll(east_side, 24, 1)
        band = jnp.where(row_ok, band, 0.0)
        rows = band[BRICK - STEPS :] if dy < 0 else band[:STEPS] if dy > 0 else band
        compact[0, place : place + rows.shape[0], :] = rows
    compact[0, ROWS:, :] = jnp.zeros((32 - ROWS, 128), F32)
    compact[1] = jnp.zeros((32, 128), F32)
    compact[1, :BRICK, :BRICK] = wet_here
    eye = lax.broadcasted_iota(jnp.int32, (COLS, 128), 1) == lax.broadcasted_iota(jnp.int32, (COLS, 128), 0)

    def spread(row, width):
        kept = jnp.where(eye[:width], jnp.broadcast_to(row, (width, 128)), 0.0)
        return jnp.broadcast_to(jnp.sum(kept, axis=1, keepdims=True), (width, 128))

    def edges(i):
        here = compact[0, pl.ds(i, 1), :]
        east[i] = spread(GAIN * jnp.minimum(here, pltpu.roll(here, 127, 1)), COLS)
        north[i] = spread(GAIN * jnp.minimum(here, compact[0, pl.ds(i + 1, 1), :]), COLS)

    pair_sum(0, ())
    for half in range(2):
        relay(half).start()
    lax.fori_loop(1, 5, send_z, 0)
    for j, half in ((5, 1), (6, 0)):
        relay(half).wait_recv()
        pair_sum(j, range(8 * half, 8 * half + 8))
        along_z(j).start()
    lax.fori_loop(0, 7, geometry, 0)
    pair(7).wait_recv()
    for r in range(BRICK):
        both[0, r] = part(7, x_hi, r) + x_in[7, r].astype(F32)
    lax.fori_loop(1, 7, add_z, 0)
    for r in range(BRICK):
        h[TOP + r, LEFT : LEFT + BRICK, :] = both[0, r] * wets[r]

    def span(i):
        dy, dx = NEIGHBOURS[i]
        tall, wide = (BRICK if dy == 0 else STEPS), (BRICK if dx == 0 else 8)
        src_y, dst_y = {-1: (TOP + BRICK - STEPS, 0), 0: (TOP, TOP), 1: (TOP, TOP + BRICK)}[dy]
        src_x, dst_x = {-1: (LEFT + BRICK - 8, 0), 0: (LEFT, LEFT), 1: (LEFT, LEFT + BRICK)}[dx]
        rows = 8 * tall
        src = (slice(src_y, src_y + tall), slice(src_x, src_x + wide), slice(None))
        dst = (slice(dst_y, dst_y + tall), slice(dst_x, dst_x + wide), slice(None))
        return dx, rows, src, dst

    def halo(i):
        dy, dx = NEIGHBOURS[i]
        _, rows, src, dst = span(i)
        to_sea, to_fault = mod(s - dy, SEA), mod(f - dx, FAULT)
        if dx == 0:
            return copy(h.at[src], h.at[dst], h_send.at[i], h_recv.at[i], to_sea, to_fault)
        return copy(strip_out.at[i, :rows], strip_in.at[i, :rows], h_send.at[i], h_recv.at[i], to_sea, to_fault)

    for i in range(8):
        dx, rows, src, _ = span(i)
        if dx:
            strip_out[i, :rows] = h[src].reshape(rows, MEMBERS).astype(BF16)
        halo(i).start()
    e[...] = jnp.zeros(e.shape, F32)
    n[...] = jnp.zeros(n.shape, F32)
    for d in RING:
        along_y(d, False).wait_send()
    for d in (0,) + RING:
        to_mate(d, x_mate, x_send, x_recv, False).wait_send()
        to_mate(d, core_mate, c_send, c_recv, False).wait_send()
        onward(d, False).wait_send()
    for i in range(8):
        depth_copy(i).wait_send()
    for j in range(8):
        pair(j).wait_send()
    for half in range(2):
        relay(half).wait_send()
    for j in range(1, 7):
        along_z(j).wait_send()
    for i in range(8):
        dx, rows, _, dst = span(i)
        halo(i).wait()
        if dx:
            h[dst] = strip_in[i, :rows].astype(F32).reshape(rows // 8, 8, MEMBERS)

    for step in range(STEPS):
        def rows(i, count, below):
            here = [h[i + k] for k in range(count + 1)]
            flows = [n[i + k] + (here[k + 1] - here[k]) for k in range(count)]
            eastward = [e[i + k] + (pltpu.roll(here[k], COLS - 1, 0) - here[k]) for k in range(count)]
            fluxes = [below] + [north[i + k] * flows[k] for k in range(count)]
            sideways = [east[i + k] * eastward[k] for k in range(count)]
            change = [side - pltpu.roll(side, 1, 0) for side in sideways]
            for k in range(count):
                n[i + k] = flows[k]
                e[i + k] = eastward[k]
                h[i + k] = here[k] + (change[k] + (fluxes[k + 1] - fluxes[k]))
            return fluxes[-1]

        count = ROWS - 2 - 2 * step
        flow = n[step] + (h[step + 1] - h[step])
        n[step] = flow
        below = north[step] * flow
        below = lax.fori_loop(0, count // TALL, lambda g, carry: rows(step + 1 + TALL * g, TALL, carry), below)
        if count % TALL:
            rows(ROWS - 1 - step - count % TALL, count % TALL, below)
    both[1] = h[TOP : TOP + BRICK, LEFT : LEFT + BRICK, :]


def on_device(*args):
    hbm = pl.BlockSpec(memory_space=pltpu.HBM)
    field = pltpu.VMEM((ROWS, COLS, MEMBERS), F32)
    dma = pltpu.SemaphoreType.DMA
    brick = jax.ShapeDtypeStruct((BRICK, BRICK, MEMBERS), F32)
    near = args[1].reshape(NEAR, 8, 2, BRICK, LEAF)
    made = pl.pallas_call(
        kernel,
        out_shape=pltpu.VMEM((2, BRICK, BRICK, MEMBERS), F32),
        in_specs=[hbm] * 13,
        out_specs=pl.BlockSpec(memory_space=pltpu.VMEM),
        scratch_shapes=[
            pltpu.VMEM((128, MEMBERS), BF16),
            *(pltpu.SMEM((1, 1, NEAR), kind) for kind in (jnp.int32, jnp.int32, F32)),
            *(pltpu.SMEM((1, 1, FAR), kind) for kind in (jnp.int32, jnp.int32, jnp.int32, F32)),
            pltpu.VMEM((BRICK, BRICK), F32),
            pltpu.VMEM((BRICK, BRICK), jnp.int32),
            pltpu.VMEM((LEAVES, LEAF, MEMBERS), BF16),
            pltpu.VMEM((FAR, 2, LEAF // 2, RANK), BF16),
            pltpu.VMEM((2, NEAR, 8, BRICK, LEAF), BF16),
            pltpu.VMEM((FAR, RANK, LEAF), BF16),
            pltpu.VMEM((FAR, RANK, LEAF), BF16),
            pltpu.VMEM((FAR, RANK, MEMBERS), BF16),
            pltpu.VMEM((1 + NEAR + FAR, 2, LEAF // 2, MEMBERS), F32),
            pltpu.SMEM((1 + NEAR + FAR,), jnp.int32),
            pltpu.SMEM((LEAVES,), jnp.int32),
            pltpu.VMEM((8, BRICK, BRICK, MEMBERS), BF16),
            pltpu.VMEM((8, BRICK, BRICK, MEMBERS), BF16),
            pltpu.VMEM((7, BRICK, BRICK, MEMBERS), BF16),
            pltpu.VMEM((7, BRICK, BRICK, MEMBERS), BF16),
            pltpu.VMEM((9, BRICK, 128), F32),
            pltpu.VMEM((2, 32, 128), F32),
            pltpu.VMEM((21, BRICK, MEMBERS), F32),
            pltpu.VMEM((8, 8 * BRICK, MEMBERS), BF16), pltpu.VMEM((8, 8 * BRICK, MEMBERS), BF16),
            field, field, field, field, field,
            dma((14,)),
            dma((8,)), dma((8,)), dma((8,)), dma((8,)), dma((8,)), dma((8,)), dma((8,)), dma((8,)),
            dma((8,)), dma((8,)),
            dma((8,)), dma((8,)), dma((8,)), dma((8,)), dma((8,)), dma((8,)),
        ],
        compiler_params=pltpu.CompilerParams(
            collective_id=0, has_side_effects=True, vmem_limit_bytes=62 * 2**20
        ),
        name="forecast",
    )(args[0], near, *args[2:])
    return made[0], made[1]


def solution(mesh):
    blocks = P("sea", "fault", None, None, None)
    lists = P("sea", "fault", None)
    cells = P("sea", "fault")
    return jax.shard_map(
        on_device,
        mesh=mesh,
        in_specs=(
            P(("fault", "sea"), None), blocks, lists, lists, lists, blocks, blocks, lists, lists, lists, lists, cells, cells,
        ),
        out_specs=(lists, lists),
        check_vma=False,
    )
```
